32 devices in a mesh: layer: 16 (over z, x, core), dp: 2 (over y).
Axes of the slice: x: 2, y: 2, z: 4, core: 2. Of those that a mesh axis runs over, the one named last changes fastest.
Arguments:
- activations: bfloat16 [16, 256, 8192], P('layer', 'dp'), may hold values from -6 to 6
- gradients: bfloat16 [16, 256, 14336], P('layer', 'dp'), may hold values from -6 to 6
- input_factor: bfloat16 [16, 8192, 256], P('layer', 'dp'), may hold values from -0.0625 to 0.0625
- output_factor: bfloat16 [16, 14336, 256], P('layer', 'dp'), may hold values from -0.046875 to 0.046875
- lengths: int32 [8], P('dp'), may hold values from 1 to 32, 160 in all
Outputs:
- influence: float32 [8, 8], P('dp')
The draws below stay inside these ranges and needn't reach their ends.
Inputs may be any that keep to these rules, and one draw needn't show every extreme that they name: `lengths`: each sequence's live tokens fill the front of its slots; the counts sum to 160 and one sequence fills all 32 slots.
All inputs are finite; a program needn't handle non-finite values. No bound on the sum of `lengths` on one device may be relied on, other than what follows from the above.
Results may differ from the reference program's by a relative error of at most 0.0003.
Values may be sent and summed in bfloat16 or wider, within the bound.
No kernel may reach another device: no remote copies, remote signals or barrier semaphores. Data moves between devices by JAX's collectives and lax.ppermute only.
A program may use at most 64 MiB of HBM per device.

```python
import math
import jax
import jax.numpy as jnp
import numpy as np
from jax import lax

D = 8192
RANK = 32
QUERIES = 8
SLOT = 32
TILE = 14336
BLOCKS = 16
SEQS = 8
TOKENS = 256


def block_levels(own_key, dims, cuts, smallest, high):
    def one(dim, shards_of):
        draws = jax.random.uniform(jax.random.fold_in(jax.random.fold_in(own_key, 6), dim), (shards_of,), jnp.float32, smallest / len(cuts), high / len(cuts))
        return jnp.repeat(jnp.exp(draws), dims[dim] // shards_of).reshape((-1,) + (1,) * (len(dims) - dim - 1))

    level = one(*cuts[0])
    for cut in cuts[1:]:
        level = level * one(*cut)
    return level


def length_profile(number_of, total, most, skew):
    loads = [(1 << 20) // math.isqrt(grade ** skew) + 1 for grade in range(2, number_of + 1)]
    surplus, given = total - most - (number_of - 1), [1] * (number_of - 1)
    while surplus > 0:
        candidates = [i for i in range(number_of - 1) if given[i] < most]
        pool, remaining = sum([loads[i] for i in candidates]), surplus
        for i in candidates:
            extra = min(most - given[i], max(1, remaining * loads[i] // pool), surplus)
            given[i] = given[i] + extra
            surplus = surplus - extra
    return np.array([most] + given)


def ragged_sizes(key, amount, total, most, slope):
    if amount == 2:
        one = jax.random.randint(key, (), max(1, total - most), min(most, total - 1) + 1)
        return jnp.stack([one, total - one])
    sizes = jnp.asarray(length_profile(amount, total, most, slope), jnp.int32)
    twos = (amount - 1) // 2
    donor, sink = sizes[1:1 + 2 * twos:2], sizes[2:2 + 2 * twos:2]
    slack = jnp.minimum(donor - 1, most - sink)
    shifted = jax.random.randint(jax.random.fold_in(key, 1), (twos,), 0, 1 << 20) % (slack + 1)
    sizes = sizes.at[1:1 + 2 * twos:2].set(donor - shifted).at[2:2 + 2 * twos:2].set(sink + shifted)
    return sizes[jax.random.permutation(jax.random.fold_in(key, 2), amount)]


def noise(key, shape, deviation, most, split=(), held_as=jnp.bfloat16):
    factor_of = block_levels(key, shape, split, -0.22, 0.18) if split else 1.0
    entries = jax.random.normal(key, shape, jnp.float32) * deviation * factor_of
    return jnp.minimum(jnp.maximum(entries, -most), most).astype(held_as)


def setup_inputs(seed: int = 0) -> dict:
    streams_of = jax.random.split(jax.random.key(seed), 6)
    activations = noise(streams_of[0], (BLOCKS, TOKENS, D), 1.0, 6.0, ((0, 16), (1, 2)))
    gradients = noise(streams_of[1], (BLOCKS, TOKENS, TILE), 1.0, 6.0, ((0, 16), (1, 2)))
    input_factor = noise(streams_of[2], (BLOCKS, D, QUERIES * RANK), D ** -0.5, 0.0625, ((0, 16), (1, 2)))
    output_factor = noise(streams_of[3], (BLOCKS, TILE, QUERIES * RANK), TILE ** -0.5, 0.046875, ((0, 16), (1, 2)))
    lengths = ragged_sizes(streams_of[4], SEQS, 5 * SEQS * SLOT // 8, SLOT, 0).astype(jnp.int32)
    return {"activations": activations, "gradients": gradients, "input_factor": input_factor, "output_factor": output_factor, "lengths": lengths}


def live_tokens(lengths, count):
    position = jnp.arange(count, dtype=jnp.int32)
    sequence = position // SLOT
    owners = sequence[:, None] == jnp.arange(lengths.shape[0], dtype=jnp.int32)[None, :]
    limit = lax.optimization_barrier(jnp.sum(jnp.where(owners, lengths[None, :], 0), axis=1))
    return (position % SLOT < limit).astype(jnp.float32)

def block_scores(block):
    inputs, grads, in_factor, out_factor = block
    projected_in = jnp.dot(inputs, in_factor, preferred_element_type=jnp.float32)
    projected_out = jnp.dot(grads, out_factor, preferred_element_type=jnp.float32)
    return lax.optimization_barrier(jnp.sum((projected_in * projected_out).reshape(TOKENS, QUERIES, RANK), axis=2))

def reference(activations, gradients, input_factor, output_factor, lengths):
    scores = lax.map(block_scores, (activations, gradients, input_factor, output_factor))
    total = lax.optimization_barrier(jnp.sum(scores, axis=0))
    live = live_tokens(lengths, TOKENS)
    per_sequence = lax.optimization_barrier(jnp.sum((total * live[:, None]).reshape(SEQS, SLOT, QUERIES), axis=1))
    return per_sequence / jnp.float32(math.sqrt(RANK * SLOT * BLOCKS))
```

```python
import functools
import math

import jax
import jax.numpy as jnp
from jax import lax
from jax.experimental import pallas as pl
from jax.experimental.pallas import tpu as pltpu
from jax.sharding import PartitionSpec as P

RANK = 32
QUERIES = 8
SLOT = 32
STEP = 8
WIDE = 512
SWAP = [(0, 1), (1, 0)]


def live_tokens(lengths, count):
    position = jnp.arange(count, dtype=jnp.int32)
    sequence = position // SLOT
    owners = sequence[:, None] == jnp.arange(lengths.shape[0], dtype=jnp.int32)[None, :]
    limit = jnp.sum(jnp.where(owners, lengths[None, :], 0), axis=1)
    return (position % SLOT < limit).astype(jnp.float32)


def rank_sum(first, second):
    return jnp.sum((first * second).reshape(first.shape[0], QUERIES, RANK), axis=2)


def gathered_scores(activations, gradients, input_factor, output_factor, lengths):
    tokens = activations.shape[1]
    projected_in = jnp.dot(
        activations[0],
        lax.all_gather(input_factor, "dp", axis=1, tiled=True)[0],
        preferred_element_type=jnp.float32,
    )
    projected_out = jnp.dot(
        gradients[0],
        lax.all_gather(output_factor, "dp", axis=1, tiled=True)[0],
        preferred_element_type=jnp.float32,
    )
    token_score = rank_sum(projected_out, projected_in)
    live = live_tokens(lengths, tokens)
    return jnp.sum(
        (token_score * live[:, None]).reshape(lengths.shape[0], SLOT, QUERIES), axis=1
    )


def selection(lengths_ref, sequences, rows, tokens):
    row = lax.broadcasted_iota(jnp.int32, (rows, tokens), 0)
    slot = lax.broadcasted_iota(jnp.int32, (rows, tokens), 1)
    picked = jnp.zeros((rows, tokens), jnp.bool_)
    before = jnp.int32(0)
    for s in range(sequences):
        length = lengths_ref[s]
        inside = slot - s * SLOT
        picked |= (inside >= 0) & (inside < length) & (row == before + inside)
        before += length
    return jnp.where(picked, 1.0, 0.0).astype(jnp.bfloat16)


VMEM = pl.BlockSpec(memory_space=pltpu.VMEM)
SMEM = pl.BlockSpec(memory_space=pltpu.SMEM)
HBM = pl.BlockSpec(memory_space=pl.ANY)


def limit(mib):
    return pltpu.CompilerParams(vmem_limit_bytes=mib * 1024 * 1024)


def fetch_half(half, ref, buf, sems):
    width = buf.shape[1]
    piece = width // 2
    copies = []
    for p in range(2):
        start = pl.multiple_of(half * width + p * piece, 128)
        copy = pltpu.make_async_copy(
            ref.at[:, pl.ds(start, piece)], buf.at[:, pl.ds(p * piece, piece)], sems.at[p]
        )
        copy.start()
        copies.append((copy, p * piece, piece))
    return copies


def half_scratch(tokens, width):
    return [pltpu.VMEM((tokens, width), jnp.bfloat16), pltpu.SemaphoreType.DMA((2,))]


def pick(select, block):
    return jnp.dot(select, block, preferred_element_type=jnp.float32).astype(jnp.bfloat16)


def first_kernel(total, bounds, half_ref, lengths_ref, act_ref, out, which_ref, buf, sems):
    copies = fetch_half(half_ref[0], act_ref, buf, sems)
    sequences = lengths_ref.shape[0]
    live = jnp.int32(0)
    for s in range(sequences):
        live += lengths_ref[s]
    most = jnp.maximum(live, total - live)
    which = jnp.int32(0)
    for bound in bounds:
        which += (most > bound).astype(jnp.int32)
    which_ref[0] = which
    select = selection(lengths_ref, sequences, out.shape[0], buf.shape[0])
    for copy, start, piece in copies:
        copy.wait()
        out[:, start : start + piece] = pick(select, buf[:, start : start + piece])


def first_rows(rows, total, bounds, half, lengths, act):
    tokens, width = act.shape[0], act.shape[1] // 2
    return pl.pallas_call(
        functools.partial(first_kernel, total, bounds),
        out_shape=[
            jax.ShapeDtypeStruct((rows, width), jnp.bfloat16),
            jax.ShapeDtypeStruct((1,), jnp.int32),
        ],
        in_specs=[SMEM, SMEM, HBM],
        out_specs=[VMEM, SMEM],
        scratch_shapes=half_scratch(tokens, width),
        compiler_params=limit(8),
    )(half, lengths, act)


def rest_kernel(chunks, extra, half_ref, lengths_ref, act_ref, grad_ref, *rest):
    outs, (a_buf, a_sems, g_buf, g_sems) = rest[:-4], rest[-4:]
    half = half_ref[0]
    g_copies = fetch_half(half, grad_ref, g_buf, g_sems)
    sequences, tokens, first = lengths_ref.shape[0], g_buf.shape[0], sum(chunks)
    select = selection(lengths_ref, sequences, first + extra, tokens)
    a_wide = a_buf.shape[1]
    if extra:
        for copy, start, piece in fetch_half(half, act_ref, a_buf, a_sems):
            copy.wait()
            outs[-1][:, start : start + piece] = pick(select[first:], a_buf[:, start : start + piece])
    for copy, start, piece in g_copies:
        copy.wait()

        def block(i, _, start=start):
            at = pl.multiple_of(start + i * WIDE, WIDE)
            packed = pick(select, g_buf[:, pl.ds(at, WIDE)])
            row = 0
            for out, size in zip(outs, chunks):
                out[:, pl.ds(at, WIDE)] = packed[row : row + size]
                row += size
            if extra:
                outs[-1][:, pl.ds(a_wide + at, WIDE)] = packed[row:]
            return 0

        lax.fori_loop(0, piece // WIDE, block, 0)


def rest_rows(chunks, extra, half, lengths, act, grad):
    tokens, a_wide, g_wide = act.shape[0], act.shape[1] // 2, grad.shape[1] // 2
    shapes = [(n, g_wide) for n in chunks] + ([(extra, a_wide + g_wide)] if extra else [])
    return pl.pallas_call(
        functools.partial(rest_kernel, chunks, extra),
        out_shape=[jax.ShapeDtypeStruct(shape, jnp.bfloat16) for shape in shapes],
        in_specs=[SMEM, SMEM, HBM, HBM],
        out_specs=[VMEM] * len(shapes),
        scratch_shapes=half_scratch(tokens, a_wide) + half_scratch(tokens, g_wide),
        compiler_params=limit(16),
    )(half, lengths, act, grad)


def own_kernel(half_ref, lengths_ref, act_ref, grad_ref, f_in, f_out, out, a_buf, a_sems, g_buf, g_sems):
    sides = (
        (fetch_half(half_ref[0], act_ref, a_buf, a_sems), a_buf, f_in),
        (fetch_half(half_ref[0], grad_ref, g_buf, g_sems), g_buf, f_out),
    )
    rows, columns = out.shape[0], f_in.shape[1]
    select = selection(lengths_ref, lengths_ref.shape[0], rows, a_buf.shape[0])
    for side, (copies, buf, factor) in enumerate(sides):
        total = jnp.zeros((rows, columns), jnp.float32)
        for copy, start, piece in copies:
            copy.wait()

            def block(i, total, buf=buf, start=start, factor=factor):
                at = pl.multiple_of(start + i * WIDE, WIDE)
                packed = pick(select, buf[:, pl.ds(at, WIDE)])
                return total + jnp.dot(
                    packed, factor[pl.ds(at, WIDE), :], preferred_element_type=jnp.float32
                )

            total = lax.fori_loop(0, piece // WIDE, block, total)
        out[:, side * columns : (side + 1) * columns] = total


def own_part(rows, half, lengths, act, grad, f_in, f_out):
    tokens, columns = act.shape[0], f_in.shape[1]
    return pl.pallas_call(
        own_kernel,
        out_shape=jax.ShapeDtypeStruct((rows, 2 * columns), jnp.float32),
        in_specs=[SMEM, SMEM, HBM, HBM, VMEM, VMEM],
        out_specs=VMEM,
        scratch_shapes=half_scratch(tokens, f_in.shape[0]) + half_scratch(tokens, f_out.shape[0]),
        compiler_params=limit(16),
    )(half, lengths, act, grad, f_in, f_out)


def project_kernel(x_ref, *refs):
    factors, out = refs[:-1], refs[-1]
    base = 0
    for side, factor in enumerate(factors):
        depth, columns = factor.shape
        out[:, side * columns : (side + 1) * columns] = jnp.dot(
            x_ref[:, base : base + depth], factor[...], preferred_element_type=jnp.float32
        )
        base += depth


def project(x, *factors):
    columns = sum(f.shape[1] for f in factors)
    return pl.pallas_call(
        project_kernel,
        out_shape=jax.ShapeDtypeStruct((x.shape[0], columns), jnp.float32),
        in_specs=[VMEM] * (1 + len(factors)),
        out_specs=VMEM,
        compiler_params=limit(8),
    )(x, *factors)


def score_kernel(spans, lengths_ref, own, *rest):
    backs, out_ref = rest[:-1], rest[-1]
    columns, sequences = QUERIES * RANK, lengths_ref.shape[0]
    sums = [jnp.zeros((1, columns), jnp.float32) for _ in range(sequences)]
    for first, size, sides in spans:
        rows = slice(first, first + size)
        total = [
            own[rows, side * columns : (side + 1) * columns]
            + backs[which][at : at + size, from_column : from_column + columns]
            for side, (which, at, from_column) in enumerate(sides)
        ]
        product = total[0] * total[1]
        row = first + lax.broadcasted_iota(jnp.int32, (size, columns), 0)
        before = jnp.int32(0)
        for s in range(sequences):
            after = before + lengths_ref[s]
            mine = (row >= before) & (row < after)
            sums[s] += jnp.sum(jnp.where(mine, product, 0.0), axis=0, keepdims=True)
            before = after
    total = jnp.concatenate(sums, axis=0)
    out_ref[...] = jnp.concatenate(
        [jnp.sum(total[:, q * RANK : (q + 1) * RANK], axis=1, keepdims=True) for q in range(QUERIES)],
        axis=1,
    )


def score(spans, lengths, own, back):
    return pl.pallas_call(
        functools.partial(score_kernel, spans),
        out_shape=jax.ShapeDtypeStruct((lengths.shape[0], QUERIES), jnp.float32),
        in_specs=[SMEM, VMEM] + [VMEM] * len(back),
        out_specs=VMEM,
        compiler_params=limit(4),
    )(lengths, own, *back)


def split_rows(rows):
    tail = [24, 8]
    return [rows - sum(tail)] + tail


def swap(x):
    return lax.ppermute(x, "dp", SWAP)


def swapped_scores(extra, first, half, other, act, grad, f_in, f_out, lengths):
    rows, columns = first.shape[0], f_in.shape[1]
    chunks = split_rows(rows)
    first_in = swap(first)
    sent = rest_rows(chunks, extra, other, lengths, act, grad)
    own = own_part(rows + extra, half, lengths, act, grad, f_in, f_out)
    groups = [(x, at, (f_out,)) for x, at in zip(sent, [sum(chunks[:i]) for i in range(len(chunks))])]
    if extra:
        groups.append((sent[-1], rows, (f_in, f_out)))
    groups.sort(key=lambda group: -group[0].size)
    arrived = [swap(x) for x, _, _ in groups]
    first_in, own = lax.optimization_barrier((first_in, own))
    made = project(first_in, f_in)
    back, spans = [swap(made)], []
    for x, (_, at, factors) in zip(arrived, groups):
        x, made = lax.optimization_barrier((x, made))
        made = project(x, *factors)
        here = len(back)
        sides = ((here, 0, 0), (here, 0, columns)) if len(factors) == 2 else ((0, at, 0), (here, 0, 0))
        spans.append((at, x.shape[0], sides))
        back.append(swap(made))
    return score(spans, lengths, own, back)


def layer_sum(x):
    size = lax.axis_size("layer")
    if size & (size - 1):
        return lax.psum(x, "layer")
    step = 1
    while step < size:
        x = x + lax.ppermute(x, "layer", [(i, i ^ step) for i in range(size)])
        step *= 2
    return x


def shards(activations, gradients, input_factor, output_factor, lengths):
    tokens = activations.shape[1]
    parts = lax.axis_size("dp")
    widths = (input_factor.shape[1], output_factor.shape[1])
    if parts == 2 and all(w % (2 * WIDE) == 0 for w in widths):
        act, grad, f_in, f_out = (x[0] for x in (activations, gradients, input_factor, output_factor))
        total = 5 * parts * tokens // 8
        rows = (total // 2 + STEP - 1) // STEP * STEP
        half = lax.axis_index("dp")[None]
        bounds = list(range(rows, tokens, STEP))
        first, which = first_rows(rows, total, bounds, 1 - half, lengths, act)
        per_sequence = lax.switch(
            which[0],
            [functools.partial(swapped_scores, extra) for extra in range(0, tokens - rows + 1, STEP)],
            *(first, half, 1 - half, act, grad, f_in, f_out, lengths),
        )
    else:
        per_sequence = gathered_scores(activations, gradients, input_factor, output_factor, lengths)
    blocks = lax.axis_size("layer")
    return layer_sum(per_sequence) / jnp.float32(math.sqrt(RANK * SLOT * blocks))


def solution(mesh):
    in_specs = (
        P("layer", "dp", None),
        P("layer", "dp", None),
        P("layer", "dp", None),
        P("layer", "dp", None),
        P("dp"),
    )
    out_specs = P("dp", None)
    return jax.shard_map(shards, mesh=mesh, in_specs=in_specs, out_specs=out_specs, check_vma=False)
```

```python
import functools
import math

import jax
import jax.numpy as jnp
from jax import lax
from jax.experimental import pallas as pl
from jax.experimental.pallas import tpu as pltpu
from jax.sharding import PartitionSpec as P

RANK = 32
QUERIES = 8
SLOT = 32
STEP = 8
WIDE = 512
SWAP = [(0, 1), (1, 0)]


def live_tokens(lengths, count):
    position = jnp.arange(count, dtype=jnp.int32)
    sequence = position // SLOT
    owners = sequence[:, None] == jnp.arange(lengths.shape[0], dtype=jnp.int32)[None, :]
    limit = jnp.sum(jnp.where(owners, lengths[None, :], 0), axis=1)
    return (position % SLOT < limit).astype(jnp.float32)


def rank_sum(first, second):
    return jnp.sum((first * second).reshape(first.shape[0], QUERIES, RANK), axis=2)


def gathered_scores(activations, gradients, input_factor, output_factor, lengths):
    tokens = activations.shape[1]
    projected_in = jnp.dot(
        activations[0],
        lax.all_gather(input_factor, "dp", axis=1, tiled=True)[0],
        preferred_element_type=jnp.float32,
    )
    projected_out = jnp.dot(
        gradients[0],
        lax.all_gather(output_factor, "dp", axis=1, tiled=True)[0],
        preferred_element_type=jnp.float32,
    )
    token_score = rank_sum(projected_out, projected_in)
    live = live_tokens(lengths, tokens)
    return jnp.sum(
        (token_score * live[:, None]).reshape(lengths.shape[0], SLOT, QUERIES), axis=1
    )


def selection(lengths_ref, sequences, rows, tokens):
    row = lax.broadcasted_iota(jnp.int32, (rows, tokens), 0)
    slot = lax.broadcasted_iota(jnp.int32, (rows, tokens), 1)
    picked = jnp.zeros((rows, tokens), jnp.bool_)
    before = jnp.int32(0)
    for s in range(sequences):
        length = lengths_ref[s]
        inside = slot - s * SLOT
        picked |= (inside >= 0) & (inside < length) & (row == before + inside)
        before += length
    return jnp.where(picked, 1.0, 0.0).astype(jnp.bfloat16)


VMEM = pl.BlockSpec(memory_space=pltpu.VMEM)
SMEM = pl.BlockSpec(memory_space=pltpu.SMEM)
HBM = pl.BlockSpec(memory_space=pl.ANY)


def limit(mib):
    return pltpu.CompilerParams(vmem_limit_bytes=mib * 1024 * 1024)


def fetch_half(half, ref, buf, sems):
    width = buf.shape[1]
    piece = width // 2
    copies = []
    for p in range(2):
        start = pl.multiple_of(half * width + p * piece, 128)
        copy = pltpu.make_async_copy(
            ref.at[:, pl.ds(start, piece)], buf.at[:, pl.ds(p * piece, piece)], sems.at[p]
        )
        copy.start()
        copies.append((copy, p * piece, piece))
    return copies


def half_scratch(tokens, width):
    return [pltpu.VMEM((tokens, width), jnp.bfloat16), pltpu.SemaphoreType.DMA((2,))]


def pick(select, block):
    return jnp.dot(select, block, preferred_element_type=jnp.float32).astype(jnp.bfloat16)


def first_kernel(total, bounds, lengths_ref, act_ref, out, flags_ref, buf, sems):
    copies = fetch_half(1 - lax.axis_index("dp"), act_ref, buf, sems)
    sequences = lengths_ref.shape[0]
    live = jnp.int32(0)
    for s in range(sequences):
        live += lengths_ref[s]
    most = jnp.maximum(live, total - live)
    which = jnp.int32(0)
    for bound in bounds:
        which += (most > bound).astype(jnp.int32)
    flags_ref[0] = which
    flags_ref[1] = (live > total - live).astype(jnp.int32)
    select = selection(lengths_ref, sequences, out.shape[0], buf.shape[0])
    for copy, start, piece in copies:
        copy.wait()
        out[:, start : start + piece] = pick(select, buf[:, start : start + piece])


def first_rows(total, bounds, lengths, act):
    tokens, width = act.shape[0], act.shape[1] // 2
    return pl.pallas_call(
        functools.partial(first_kernel, total, bounds),
        out_shape=[
            jax.ShapeDtypeStruct((tokens, width), jnp.bfloat16),
            jax.ShapeDtypeStruct((2,), jnp.int32),
        ],
        in_specs=[SMEM, HBM],
        out_specs=[VMEM, SMEM],
        scratch_shapes=half_scratch(tokens, width),
        compiler_params=limit(8),
    )(lengths, act)


def blocks_of(rows, size):
    return [(at, min(size, rows - at)) for at in range(0, rows, size)]


def rest_kernel(chunks, pieces, lent, flags_ref, lengths_ref, act, f_in, grad_ref, *rest):
    outs, (buf, sems, wide) = rest[:-3], rest[-3:]
    copies = fetch_half(1 - lax.axis_index("dp"), grad_ref, buf, sems)
    base, extra, width = sum(chunks), sum(pieces), act.shape[1]
    select = selection(lengths_ref, lengths_ref.shape[0], base + extra, buf.shape[0])
    lender = (flags_ref[1] == 0) & (lent > 0)
    if lent:

        @pl.when(lender)
        def _():
            column = 0
            for at, size in blocks_of(base, extra):
                wide[:size, column : column + lent] = act[at : at + size, :lent]
                column += lent
            for at, size in blocks_of(lent, extra):
                wide[:size, column : column + f_in.shape[1]] = f_in[at : at + size, :]
                column += f_in.shape[1]

    if extra:

        @pl.when(jnp.logical_not(lender))
        def _():
            wide[:, : width - lent] = act[base : base + extra, lent:]

    for copy, start, piece in copies:
        copy.wait()

        def block(i, _, start=start):
            at = pl.multiple_of(start + i * WIDE, WIDE)
            packed = pick(select, buf[:, pl.ds(at, WIDE)])
            row = 0
            for out, size in zip(outs, chunks):
                out[:, pl.ds(at, WIDE)] = packed[row : row + size]
                row += size
            if extra:

                @pl.when(jnp.logical_not(lender))
                def _():
                    wide[:, pl.ds(width - lent + at, WIDE)] = packed[row:]

            return 0

        lax.fori_loop(0, piece // WIDE, block, 0)
    row = 0
    for out, size in zip(outs[len(chunks) :], pieces):
        out[...] = wide[row : row + size, :]
        row += size


def rest_rows(chunks, pieces, lent, flags, lengths, act, f_in, grad):
    tokens, a_wide, g_wide = grad.shape[0], act.shape[1], grad.shape[1] // 2
    shapes = [(n, g_wide) for n in chunks] + [(n, a_wide - lent + g_wide) for n in pieces]
    wide = (sum(pieces), a_wide - lent + g_wide) if pieces else (8, 128)
    return pl.pallas_call(
        functools.partial(rest_kernel, chunks, pieces, lent),
        out_shape=[jax.ShapeDtypeStruct(shape, jnp.bfloat16) for shape in shapes],
        in_specs=[SMEM, SMEM, VMEM, VMEM, HBM],
        out_specs=[VMEM] * len(shapes),
        scratch_shapes=half_scratch(tokens, g_wide) + [pltpu.VMEM(wide, jnp.bfloat16)],
        compiler_params=limit(16),
    )(flags, lengths, act, f_in, grad)


def own_kernel(lengths_ref, act_ref, grad_ref, f_in, f_out, out, a_buf, a_sems, g_buf, g_sems):
    half = lax.axis_index("dp")
    sides = (
        (fetch_half(half, act_ref, a_buf, a_sems), a_buf, f_in),
        (fetch_half(half, grad_ref, g_buf, g_sems), g_buf, f_out),
    )
    rows, columns = out.shape[0], f_in.shape[1]
    select = selection(lengths_ref, lengths_ref.shape[0], rows, a_buf.shape[0])
    for side, (copies, buf, factor) in enumerate(sides):
        total = jnp.zeros((rows, columns), jnp.float32)
        for copy, start, piece in copies:
            copy.wait()

            def block(i, total, buf=buf, start=start, factor=factor):
                at = pl.multiple_of(start + i * WIDE, WIDE)
                packed = pick(select, buf[:, pl.ds(at, WIDE)])
                return total + jnp.dot(
                    packed, factor[pl.ds(at, WIDE), :], preferred_element_type=jnp.float32
                )

            total = lax.fori_loop(0, piece // WIDE, block, total)
        out[:, side * columns : (side + 1) * columns] = total


def own_part(rows, lengths, act, grad, f_in, f_out):
    tokens, columns = act.shape[0], f_in.shape[1]
    return pl.pallas_call(
        own_kernel,
        out_shape=jax.ShapeDtypeStruct((rows, 2 * columns), jnp.float32),
        in_specs=[SMEM, HBM, HBM, VMEM, VMEM],
        out_specs=VMEM,
        scratch_shapes=half_scratch(tokens, f_in.shape[0]) + half_scratch(tokens, f_out.shape[0]),
        compiler_params=limit(16),
    )(lengths, act, grad, f_in, f_out)


def encode(out, x):
    rows = x.shape[0]
    most = jnp.max(jnp.abs(x), axis=0, keepdims=True)
    power = jnp.ceil(jnp.log2(jnp.maximum(most, 2.0**-100)))
    whole = jnp.clip(jnp.round(x * jnp.exp2(15.0 - power)), -32767.0, 32767.0)
    out[:rows, :] = whole.astype(jnp.int32).astype(jnp.int16)
    out[rows:, :] = jnp.broadcast_to(power, (8, x.shape[1])).astype(jnp.int32).astype(jnp.int16)


def decode(ref, at, size, column, columns):
    rows, span = ref.shape[0] - 8, slice(column, column + columns)
    power = ref[rows : rows + 8, span].astype(jnp.int32).astype(jnp.float32)[:1]
    return ref[at : at + size, span].astype(jnp.int32).astype(jnp.float32) * jnp.exp2(power - 15.0)


def first_project_kernel(lent, x_ref, f_in, out):
    total = jnp.dot(x_ref[...], f_in[lent:, :], preferred_element_type=jnp.float32)
    if lent:
        out[...] = total
    else:
        encode(out, total)


def first_project(lent, x, f_in):
    rows, columns = x.shape[0], f_in.shape[1]
    return pl.pallas_call(
        functools.partial(first_project_kernel, lent),
        out_shape=jax.ShapeDtypeStruct((rows, columns), jnp.float32)
        if lent
        else jax.ShapeDtypeStruct((rows + 8, columns), jnp.int16),
        in_specs=[VMEM] * 2,
        out_specs=VMEM,
        compiler_params=limit(8),
    )(x, f_in)


def project_kernel(x_ref, f_out, out):
    out[...] = jnp.dot(x_ref[...], f_out[...], preferred_element_type=jnp.float32)


def project(x, f_out):
    rows, columns = x.shape[0], f_out.shape[1]
    return pl.pallas_call(
        project_kernel,
        out_shape=jax.ShapeDtypeStruct((rows, columns), jnp.float32),
        in_specs=[VMEM] * 2,
        out_specs=VMEM,
        compiler_params=limit(8),
    )(x, f_out)


def plain_kernel(x_ref, f_in, f_out, out):
    depth = f_in.shape[0]
    inner = jnp.dot(x_ref[:, :depth], f_in[...], preferred_element_type=jnp.float32)
    outer = jnp.dot(x_ref[:, depth:], f_out[...], preferred_element_type=jnp.float32)
    encode(out, jnp.concatenate([inner, outer], axis=1))


def plain_project(x, f_in, f_out):
    return pl.pallas_call(
        plain_kernel,
        out_shape=jax.ShapeDtypeStruct((x.shape[0] + 8, 2 * f_in.shape[1]), jnp.int16),
        in_specs=[VMEM] * 3,
        out_specs=VMEM,
        compiler_params=limit(8),
    )(x, f_in, f_out)


def extra_kernel(lent, base, flags_ref, made, act, f_in, f_out, *rest):
    pieces, (back, added, total, a_buf, f_buf, x_ref) = rest[:-6], rest[-6:]
    extra, (width, columns) = x_ref.shape[0], f_in.shape
    rows = base + extra
    row = 0
    for piece in pieces:
        x_ref[row : row + piece.shape[0], :] = piece[...]
        row += piece.shape[0]
    borrower = flags_ref[1] == 1

    @pl.when(borrower)
    def _():
        column = 0
        for at, size in blocks_of(base, extra):
            a_buf[at : at + size, :] = x_ref[:size, column : column + lent]
            column += lent
        for at, size in blocks_of(lent, extra):
            f_buf[at : at + size, :] = x_ref[:size, column : column + columns]
            column += columns
        total[:base, :] = made[...] + jnp.dot(
            a_buf[...], f_in[:lent, :], preferred_element_type=jnp.float32
        )
        total[base:, :] = jnp.zeros((2 * extra, columns), jnp.float32)
        added[...] = jnp.dot(act[:rows, :lent], f_buf[...], preferred_element_type=jnp.float32)

    @pl.when(jnp.logical_not(borrower))
    def _():
        total[:base, :] = made[...]
        total[base:rows, :] = jnp.dot(
            x_ref[:, : width - lent], f_in[lent:, :], preferred_element_type=jnp.float32
        )
        total[rows:, :] = jnp.dot(
            x_ref[:, width - lent :], f_out[...], preferred_element_type=jnp.float32
        )
        added[...] = jnp.zeros((rows, columns), jnp.float32)

    encode(back, total[...])


def extra_rows(lent, flags, made, pieces, act, f_in, f_out):
    base, extra, columns = made.shape[0], sum(x.shape[0] for x in pieces), f_in.shape[1]
    return pl.pallas_call(
        functools.partial(extra_kernel, lent, base),
        out_shape=[
            jax.ShapeDtypeStruct((base + 2 * extra + 8, columns), jnp.int16),
            jax.ShapeDtypeStruct((base + extra, columns), jnp.float32),
        ],
        in_specs=[SMEM] + [VMEM] * (4 + len(pieces)),
        out_specs=[VMEM, VMEM],
        scratch_shapes=[
            pltpu.VMEM((base + 2 * extra, columns), jnp.float32),
            pltpu.VMEM((base, lent), jnp.bfloat16),
            pltpu.VMEM((lent, columns), jnp.bfloat16),
            pltpu.VMEM((extra, pieces[0].shape[1]), jnp.bfloat16),
        ],
        compiler_params=limit(8),
    )(flags, made, act, f_in, f_out, *pieces)


def score_kernel(spans, lengths_ref, *rest):
    arrays, out_ref = rest[:-1], rest[-1]
    columns, sequences = QUERIES * RANK, lengths_ref.shape[0]
    sums = [jnp.zeros((1, columns), jnp.float32) for _ in range(sequences)]
    for first, size, sides in spans:
        total = [
            sum(
                decode(arrays[which], at, size, column, columns)
                if arrays[which].dtype == jnp.int16
                else arrays[which][at : at + size, column : column + columns]
                for which, at, column in parts
            )
            for parts in sides
        ]
        product = total[0] * total[1]
        row = first + lax.broadcasted_iota(jnp.int32, (size, columns), 0)
        before = jnp.int32(0)
        for s in range(sequences):
            after = before + lengths_ref[s]
            mine = (row >= before) & (row < after)
            sums[s] += jnp.sum(jnp.where(mine, product, 0.0), axis=0, keepdims=True)
            before = after
    total = jnp.concatenate(sums, axis=0)
    out_ref[...] = jnp.concatenate(
        [jnp.sum(total[:, q * RANK : (q + 1) * RANK], axis=1, keepdims=True) for q in range(QUERIES)],
        axis=1,
    )


def score(spans, lengths, arrays):
    return pl.pallas_call(
        functools.partial(score_kernel, spans),
        out_shape=jax.ShapeDtypeStruct((lengths.shape[0], QUERIES), jnp.float32),
        in_specs=[SMEM] + [VMEM] * len(arrays),
        out_specs=VMEM,
        compiler_params=limit(4),
    )(lengths, *arrays)


def lendable(base, extra, columns, a_wide, g_wide):
    best = 0
    for lent in range(128, a_wide, 128):
        used = len(blocks_of(base, extra)) * lent + len(blocks_of(lent, extra)) * columns
        if used <= a_wide - lent + g_wide:
            best = lent
    return best


def swap(x):
    return lax.ppermute(x, "dp", SWAP)


def swapped_scores(rows, base, lent, chunks, flags, lengths, packed, act, grad, f_in, f_out):
    columns, extra = f_in.shape[1], rows - base
    first = swap(packed[:base, lent:])
    sent = rest_rows(chunks, [extra], lent, flags, lengths, packed, f_in, grad)
    groups = list(zip(sent, [sum(chunks[:i]) for i in range(len(chunks))] + [base]))
    groups.sort(key=lambda group: -group[0].size)
    arrived = [swap(x) for x, _ in groups]
    own = own_part(rows, lengths, act, grad, f_in, f_out)
    first, own = lax.optimization_barrier((first, own))
    done = made = first_project(lent, first, f_in)
    arrays, spans, in_parts = [own], [], [0]
    if not lent:
        in_parts.append(len(arrays))
        arrays.append(swap(made))
    for x, (_, at) in zip(arrived, groups):
        x, done = lax.optimization_barrier((x, done))
        here = len(arrays)
        if at < base:
            done = project(x, f_out)
            spans.append((at, x.shape[0], (here, 0, 0)))
        elif not lent:
            done = plain_project(x, f_in, f_out)
            spans.append((at, extra, (here, 0, columns)))
        else:
            done, added = extra_rows(lent, flags, made, [x], packed, f_in, f_out)
            in_parts += [here, here + 1]
            spans.append((at, extra, (here, rows, 0)))
        arrays.append(swap(done))
        if lent and at == base:
            arrays.append(added)
    spans = [
        (
            at,
            size,
            (
                ((0, at, 0), (back[0], 0, 0))
                if at == base and not lent
                else tuple((which, at, 0) for which in in_parts),
                ((0, at, columns), back),
            ),
        )
        for at, size, back in spans
    ]
    return score(spans, lengths, arrays)


def plan(rows, even, a_wide, g_wide, columns):
    if rows <= even + STEP:
        base = even - STEP
        large = (base + STEP) // 2 // STEP * STEP
        return rows, base, 0, [large, base - large]
    large = (even * 2 // 5) // STEP * STEP
    return rows, even, lendable(even, rows - even, columns, a_wide, g_wide), [large, large, even - 2 * large]


def layer_sum(x):
    size = lax.axis_size("layer")
    if size & (size - 1):
        return lax.psum(x, "layer")
    step = 1
    while step < size:
        x = x + lax.ppermute(x, "layer", [(i, i ^ step) for i in range(size)])
        step *= 2
    return x


def shards(activations, gradients, input_factor, output_factor, lengths):
    tokens = activations.shape[1]
    parts = lax.axis_size("dp")
    widths = (input_factor.shape[1], output_factor.shape[1])
    if parts == 2 and all(w % (2 * WIDE) == 0 for w in widths):
        act, grad, f_in, f_out = (x[0] for x in (activations, gradients, input_factor, output_factor))
        total = 5 * parts * tokens // 8
        even = (total // 2 + STEP - 1) // STEP * STEP
        bounds = list(range(even, tokens, STEP))
        packed, flags = first_rows(total, bounds, lengths, act)
        plans = [plan(rows, even, *widths, f_in.shape[1]) for rows in range(even, tokens + 1, STEP)]
        per_sequence = lax.switch(
            flags[0],
            [functools.partial(swapped_scores, *p) for p in plans],
            *(flags, lengths, packed, act, grad, f_in, f_out),
        )
    else:
        per_sequence = gathered_scores(activations, gradients, input_factor, output_factor, lengths)
    blocks = lax.axis_size("layer")
    return layer_sum(per_sequence) / jnp.float32(math.sqrt(RANK * SLOT * blocks))


def solution(mesh):
    in_specs = (
        P("layer", "dp", None),
        P("layer", "dp", None),
        P("layer", "dp", None),
        P("layer", "dp", None),
        P("dp"),
    )
    out_specs = P("dp", None)
    return jax.shard_map(shards, mesh=mesh, in_specs=in_specs, out_specs=out_specs, check_vma=False)
```

```python
import functools
import math

import jax
import jax.numpy as jnp
from jax import lax
from jax.experimental import pallas as pl
from jax.experimental.pallas import tpu as pltpu
from jax.sharding import PartitionSpec as P

RANK = 32
QUERIES = 8
SLOT = 32
STEP = 8
WIDE = 512
MOST = 3
SWAP = [(0, 1), (1, 0)]


def live_tokens(lengths, count):
    position = jnp.arange(count, dtype=jnp.int32)
    sequence = position // SLOT
    owners = sequence[:, None] == jnp.arange(lengths.shape[0], dtype=jnp.int32)[None, :]
    limit = jnp.sum(jnp.where(owners, lengths[None, :], 0), axis=1)
    return (position % SLOT < limit).astype(jnp.float32)


def rank_sum(first, second):
    return jnp.sum((first * second).reshape(first.shape[0], QUERIES, RANK), axis=2)


def gathered_scores(activations, gradients, input_factor, output_factor, lengths):
    tokens = activations.shape[1]
    projected_in = jnp.dot(
        activations[0],
        lax.all_gather(input_factor, "dp", axis=1, tiled=True)[0],
        preferred_element_type=jnp.float32,
    )
    projected_out = jnp.dot(
        gradients[0],
        lax.all_gather(output_factor, "dp", axis=1, tiled=True)[0],
        preferred_element_type=jnp.float32,
    )
    token_score = rank_sum(projected_out, projected_in)
    live = live_tokens(lengths, tokens)
    return jnp.sum(
        (token_score * live[:, None]).reshape(lengths.shape[0], SLOT, QUERIES), axis=1
    )


def selection(lengths_ref, sequences, rows, tokens):
    row = lax.broadcasted_iota(jnp.int32, (rows, tokens), 0)
    slot = lax.broadcasted_iota(jnp.int32, (rows, tokens), 1)
    picked = jnp.zeros((rows, tokens), jnp.bool_)
    before = jnp.int32(0)
    for s in range(sequences):
        length = lengths_ref[s]
        inside = slot - s * SLOT
        picked |= (inside >= 0) & (inside < length) & (row == before + inside)
        before += length
    return jnp.where(picked, 1.0, 0.0).astype(jnp.bfloat16)


VMEM = pl.BlockSpec(memory_space=pltpu.VMEM)
SMEM = pl.BlockSpec(memory_space=pltpu.SMEM)
HBM = pl.BlockSpec(memory_space=pl.ANY)


def limit(mib):
    return pltpu.CompilerParams(vmem_limit_bytes=mib * 1024 * 1024)


def fetch_half(half, ref, buf, sems):
    width = buf.shape[1]
    piece = width // 2
    copies = []
    for p in range(2):
        start = pl.multiple_of(half * width + p * piece, 128)
        copy = pltpu.make_async_copy(
            ref.at[:, pl.ds(start, piece)], buf.at[:, pl.ds(p * piece, piece)], sems.at[p]
        )
        copy.start()
        copies.append((copy, p * piece, piece))
    return copies


def half_scratch(tokens, width):
    return [pltpu.VMEM((tokens, width), jnp.bfloat16), pltpu.SemaphoreType.DMA((2,))]


def pick(select, block):
    return jnp.dot(select, block, preferred_element_type=jnp.float32).astype(jnp.bfloat16)


def first_kernel(total, bounds, lengths_ref, act_ref, out, flags_ref, buf, sems):
    copies = fetch_half(1 - lax.axis_index("dp"), act_ref, buf, sems)
    sequences = lengths_ref.shape[0]
    live = jnp.int32(0)
    for s in range(sequences):
        live += lengths_ref[s]
    most = jnp.maximum(live, total - live)
    which = jnp.int32(0)
    for bound in bounds:
        which += (most > bound).astype(jnp.int32)
    flags_ref[0] = which
    flags_ref[1] = (live > total - live).astype(jnp.int32)
    select = selection(lengths_ref, sequences, out.shape[0], buf.shape[0])
    for copy, start, piece in copies:
        copy.wait()
        out[:, start : start + piece] = pick(select, buf[:, start : start + piece])


def first_rows(total, bounds, lengths, act):
    tokens, width = act.shape[0], act.shape[1] // 2
    return pl.pallas_call(
        functools.partial(first_kernel, total, bounds),
        out_shape=[
            jax.ShapeDtypeStruct((tokens, width), jnp.bfloat16),
            jax.ShapeDtypeStruct((2,), jnp.int32),
        ],
        in_specs=[SMEM, HBM],
        out_specs=[VMEM, SMEM],
        scratch_shapes=half_scratch(tokens, width),
        compiler_params=limit(8),
    )(lengths, act)


def blocks_of(rows, size):
    return [(at, min(size, rows - at)) for at in range(0, rows, size)]


def rest_kernel(chunks, pieces, lent, flags_ref, lengths_ref, act, f_in, grad_ref, *rest):
    outs, (buf, sems, wide) = rest[:-3], rest[-3:]
    copies = fetch_half(1 - lax.axis_index("dp"), grad_ref, buf, sems)
    base, extra, width = sum(chunks), sum(pieces), act.shape[1]
    select = selection(lengths_ref, lengths_ref.shape[0], base + extra, buf.shape[0])
    lender = (flags_ref[1] == 0) & (lent > 0)
    if lent:

        @pl.when(lender)
        def _():
            column = 0
            for at, size in blocks_of(base, extra):
                wide[:size, column : column + lent] = act[at : at + size, :lent]
                column += lent
            for at, size in blocks_of(lent, extra):
                wide[:size, column : column + f_in.shape[1]] = f_in[at : at + size, :]
                column += f_in.shape[1]

    if extra:

        @pl.when(jnp.logical_not(lender))
        def _():
            wide[:, : width - lent] = act[base : base + extra, lent:]

    for copy, start, piece in copies:
        copy.wait()

        def block(i, _, start=start):
            at = pl.multiple_of(start + i * WIDE, WIDE)
            packed = pick(select, buf[:, pl.ds(at, WIDE)])
            row = 0
            for out, size in zip(outs, chunks):
                out[:, pl.ds(at, WIDE)] = packed[row : row + size]
                row += size
            if extra:

                @pl.when(jnp.logical_not(lender))
                def _():
                    wide[:, pl.ds(width - lent + at, WIDE)] = packed[row:]

            return 0

        lax.fori_loop(0, piece // WIDE, block, 0)
    row = 0
    for out, size in zip(outs[len(chunks) :], pieces):
        out[...] = wide[row : row + size, :]
        row += size


def rest_rows(chunks, pieces, lent, flags, lengths, act, f_in, grad):
    tokens, a_wide, g_wide = grad.shape[0], act.shape[1], grad.shape[1] // 2
    shapes = [(n, g_wide) for n in chunks] + [(n, a_wide - lent + g_wide) for n in pieces]
    wide = (sum(pieces), a_wide - lent + g_wide) if pieces else (8, 128)
    return pl.pallas_call(
        functools.partial(rest_kernel, chunks, pieces, lent),
        out_shape=[jax.ShapeDtypeStruct(shape, jnp.bfloat16) for shape in shapes],
        in_specs=[SMEM, SMEM, VMEM, VMEM, HBM],
        out_specs=[VMEM] * len(shapes),
        scratch_shapes=half_scratch(tokens, g_wide) + [pltpu.VMEM(wide, jnp.bfloat16)],
        compiler_params=limit(16),
    )(flags, lengths, act, f_in, grad)


def own_kernel(lengths_ref, act_ref, grad_ref, f_in, f_out, out, a_buf, a_sems, g_buf, g_sems):
    half = lax.axis_index("dp")
    sides = (
        (fetch_half(half, act_ref, a_buf, a_sems), a_buf, f_in),
        (fetch_half(half, grad_ref, g_buf, g_sems), g_buf, f_out),
    )
    rows, columns = out.shape[0], f_in.shape[1]
    select = selection(lengths_ref, lengths_ref.shape[0], rows, a_buf.shape[0])
    for side, (copies, buf, factor) in enumerate(sides):
        total = jnp.zeros((rows, columns), jnp.float32)
        for copy, start, piece in copies:
            copy.wait()

            def block(i, total, buf=buf, start=start, factor=factor):
                at = pl.multiple_of(start + i * WIDE, WIDE)
                packed = pick(select, buf[:, pl.ds(at, WIDE)])
                return total + jnp.dot(
                    packed, factor[pl.ds(at, WIDE), :], preferred_element_type=jnp.float32
                )

            total = lax.fori_loop(0, piece // WIDE, block, total)
        out[:, side * columns : (side + 1) * columns] = total


def own_part(rows, lengths, act, grad, f_in, f_out):
    tokens, columns = act.shape[0], f_in.shape[1]
    return pl.pallas_call(
        own_kernel,
        out_shape=jax.ShapeDtypeStruct((rows, 2 * columns), jnp.float32),
        in_specs=[SMEM, HBM, HBM, VMEM, VMEM],
        out_specs=VMEM,
        scratch_shapes=half_scratch(tokens, f_in.shape[0]) + half_scratch(tokens, f_out.shape[0]),
        compiler_params=limit(16),
    )(lengths, act, grad, f_in, f_out)


def encode(out, x):
    rows = x.shape[0]
    most = jnp.max(jnp.abs(x), axis=0, keepdims=True)
    power = jnp.ceil(jnp.log2(jnp.maximum(most, 2.0**-100)))
    whole = jnp.clip(jnp.round(x * jnp.exp2(15.0 - power)), -32767.0, 32767.0)
    out[:rows, :] = whole.astype(jnp.int32).astype(jnp.int16)
    out[rows:, :] = jnp.broadcast_to(power, (8, x.shape[1])).astype(jnp.int32).astype(jnp.int16)


def decode(ref, at, size, column, columns):
    rows, span = ref.shape[0] - 8, slice(column, column + columns)
    power = ref[rows : rows + 8, span].astype(jnp.int32).astype(jnp.float32)[:1]
    return ref[at : at + size, span].astype(jnp.int32).astype(jnp.float32) * jnp.exp2(power - 15.0)


def first_project_kernel(lent, x_ref, f_in, out):
    total = jnp.dot(x_ref[...], f_in[lent:, :], preferred_element_type=jnp.float32)
    if lent:
        out[...] = total
    else:
        encode(out, total)


def first_project(lent, x, f_in):
    rows, columns = x.shape[0], f_in.shape[1]
    return pl.pallas_call(
        functools.partial(first_project_kernel, lent),
        out_shape=jax.ShapeDtypeStruct((rows, columns), jnp.float32)
        if lent
        else jax.ShapeDtypeStruct((rows + 8, columns), jnp.int16),
        in_specs=[VMEM] * 2,
        out_specs=VMEM,
        compiler_params=limit(8),
    )(x, f_in)


def project_kernel(x_ref, f_out, out):
    out[...] = jnp.dot(x_ref[...], f_out[...], preferred_element_type=jnp.float32)


def project(x, f_out):
    rows, columns = x.shape[0], f_out.shape[1]
    return pl.pallas_call(
        project_kernel,
        out_shape=jax.ShapeDtypeStruct((rows, columns), jnp.float32),
        in_specs=[VMEM] * 2,
        out_specs=VMEM,
        compiler_params=limit(8),
    )(x, f_out)


def plain_kernel(x_ref, f_in, f_out, out):
    depth = f_in.shape[0]
    inner = jnp.dot(x_ref[:, :depth], f_in[...], preferred_element_type=jnp.float32)
    outer = jnp.dot(x_ref[:, depth:], f_out[...], preferred_element_type=jnp.float32)
    encode(out, jnp.concatenate([inner, outer], axis=1))


def plain_project(x, f_in, f_out):
    return pl.pallas_call(
        plain_kernel,
        out_shape=jax.ShapeDtypeStruct((x.shape[0] + 8, 2 * f_in.shape[1]), jnp.int16),
        in_specs=[VMEM] * 3,
        out_specs=VMEM,
        compiler_params=limit(8),
    )(x, f_in, f_out)


def extra_kernel(lent, base, flags_ref, made, act, f_in, f_out, *rest):
    pieces, (back, added, total, a_buf, f_buf, x_ref) = rest[:-6], rest[-6:]
    extra, (width, columns) = x_ref.shape[0], f_in.shape
    rows = base + extra
    row = 0
    for piece in pieces:
        x_ref[row : row + piece.shape[0], :] = piece[...]
        row += piece.shape[0]
    borrower = flags_ref[1] == 1

    @pl.when(borrower)
    def _():
        column = 0
        for at, size in blocks_of(base, extra):
            a_buf[at : at + size, :] = x_ref[:size, column : column + lent]
            column += lent
        for at, size in blocks_of(lent, extra):
            f_buf[at : at + size, :] = x_ref[:size, column : column + columns]
            column += columns
        total[:base, :] = made[...] + jnp.dot(
            a_buf[...], f_in[:lent, :], preferred_element_type=jnp.float32
        )
        total[base:, :] = jnp.zeros((2 * extra, columns), jnp.float32)
        added[...] = jnp.dot(act[:rows, :lent], f_buf[...], preferred_element_type=jnp.float32)

    @pl.when(jnp.logical_not(borrower))
    def _():
        total[:base, :] = made[...]
        total[base:rows, :] = jnp.dot(
            x_ref[:, : width - lent], f_in[lent:, :], preferred_element_type=jnp.float32
        )
        total[rows:, :] = jnp.dot(
            x_ref[:, width - lent :], f_out[...], preferred_element_type=jnp.float32
        )
        added[...] = jnp.zeros((rows, columns), jnp.float32)

    encode(back, total[...])


def extra_rows(lent, flags, made, pieces, act, f_in, f_out):
    base, extra, columns = made.shape[0], sum(x.shape[0] for x in pieces), f_in.shape[1]
    return pl.pallas_call(
        functools.partial(extra_kernel, lent, base),
        out_shape=[
            jax.ShapeDtypeStruct((base + 2 * extra + 8, columns), jnp.int16),
            jax.ShapeDtypeStruct((base + extra, columns), jnp.float32),
        ],
        in_specs=[SMEM] + [VMEM] * (4 + len(pieces)),
        out_specs=[VMEM, VMEM],
        scratch_shapes=[
            pltpu.VMEM((base + 2 * extra, columns), jnp.float32),
            pltpu.VMEM((base, lent), jnp.bfloat16),
            pltpu.VMEM((lent, columns), jnp.bfloat16),
            pltpu.VMEM((extra, pieces[0].shape[1]), jnp.bfloat16),
        ],
        compiler_params=limit(8),
    )(flags, made, act, f_in, f_out, *pieces)


def score_kernel(spans, lengths_ref, *rest):
    arrays, out_ref = rest[:-1], rest[-1]
    columns, sequences = QUERIES * RANK, lengths_ref.shape[0]
    sums = [jnp.zeros((1, columns), jnp.float32) for _ in range(sequences)]
    for first, size, sides in spans:
        total = [
            sum(
                decode(arrays[which], at, size, column, columns)
                if arrays[which].dtype == jnp.int16
                else arrays[which][at : at + size, column : column + columns]
                for which, at, column in parts
            )
            for parts in sides
        ]
        product = total[0] * total[1]
        row = first + lax.broadcasted_iota(jnp.int32, (size, columns), 0)
        before = jnp.int32(0)
        for s in range(sequences):
            after = before + lengths_ref[s]
            mine = (row >= before) & (row < after)
            sums[s] += jnp.sum(jnp.where(mine, product, 0.0), axis=0, keepdims=True)
            before = after
    total = jnp.concatenate(sums, axis=0)
    out_ref[...] = jnp.concatenate(
        [jnp.sum(total[:, q * RANK : (q + 1) * RANK], axis=1, keepdims=True) for q in range(QUERIES)],
        axis=1,
    )


def score(spans, lengths, arrays):
    return pl.pallas_call(
        functools.partial(score_kernel, spans),
        out_shape=jax.ShapeDtypeStruct((lengths.shape[0], QUERIES), jnp.float32),
        in_specs=[SMEM] + [VMEM] * len(arrays),
        out_specs=VMEM,
        compiler_params=limit(4),
    )(lengths, *arrays)


def lendable(base, extra, columns, a_wide, g_wide):
    best = 0
    for lent in range(128, a_wide, 128):
        used = len(blocks_of(base, extra)) * lent + len(blocks_of(lent, extra)) * columns
        if used <= a_wide - lent + g_wide:
            best = lent
    return best


def swap(x):
    return lax.ppermute(x, "dp", SWAP)


def swapped_scores(rows, base, lent, chunks, flags, lengths, packed, act, grad, f_in, f_out):
    columns, extra = f_in.shape[1], rows - base
    first = swap(packed[:base, lent:])
    sent = rest_rows(chunks, [extra], lent, flags, lengths, packed, f_in, grad)
    groups = list(zip(sent, [sum(chunks[:i]) for i in range(len(chunks))] + [base]))
    groups.sort(key=lambda group: -group[0].size)
    arrived = [swap(x) for x, _ in groups]
    own = own_part(rows, lengths, act, grad, f_in, f_out)
    first, own = lax.optimization_barrier((first, own))
    done = made = first_project(lent, first, f_in)
    arrays, spans, in_parts = [own], [], [0]
    if not lent:
        in_parts.append(len(arrays))
        arrays.append(swap(made))
    for x, (_, at) in zip(arrived, groups):
        x, done = lax.optimization_barrier((x, done))
        here = len(arrays)
        if at < base:
            done = project(x, f_out)
            spans.append((at, x.shape[0], (here, 0, 0)))
        elif not lent:
            done = plain_project(x, f_in, f_out)
            spans.append((at, extra, (here, 0, columns)))
        else:
            done, added = extra_rows(lent, flags, made, [x], packed, f_in, f_out)
            in_parts += [here, here + 1]
            spans.append((at, extra, (here, rows, 0)))
        arrays.append(swap(done))
        if lent and at == base:
            arrays.append(added)
    spans = [
        (
            at,
            size,
            (
                ((0, at, 0), (back[0], 0, 0))
                if at == base and not lent
                else tuple((which, at, 0) for which in in_parts),
                ((0, at, columns), back),
            ),
        )
        for at, size, back in spans
    ]
    return score(spans, lengths, arrays)


def plan(rows, even, a_wide, g_wide, columns):
    if rows <= even + STEP:
        base = even - STEP
        large = (base + STEP) // 2 // STEP * STEP
        return rows, base, 0, [large, base - large]
    large = (even * 2 // 5) // STEP * STEP
    return rows, even, lendable(even, rows - even, columns, a_wide, g_wide), [large, large, even - 2 * large]


def layer_sum(x):
    size = lax.axis_size("layer")
    if size & (size - 1):
        return lax.psum(x, "layer")
    step = 1
    while step < size:
        x = x + lax.ppermute(x, "layer", [(i, i ^ step) for i in range(size)])
        step *= 2
    return x


def shards(activations, gradients, input_factor, output_factor, lengths):
    tokens = activations.shape[1]
    parts = lax.axis_size("dp")
    widths = (input_factor.shape[1], output_factor.shape[1])
    if parts == 2 and all(w % (2 * WIDE) == 0 for w in widths):
        act, grad, f_in, f_out = (x[0] for x in (activations, gradients, input_factor, output_factor))
        total = 5 * parts * tokens // 8
        even = (total // 2 + STEP - 1) // STEP * STEP
        sizes = [n for n in range(even, tokens, STEP) if n <= even + MOST * STEP] + [tokens]
        bounds = sizes[:-1]
        packed, flags = first_rows(total, bounds, lengths, act)
        plans = [plan(rows, even, *widths, f_in.shape[1]) for rows in sizes]
        per_sequence = lax.switch(
            flags[0],
            [functools.partial(swapped_scores, *p) for p in plans],
            *(flags, lengths, packed, act, grad, f_in, f_out),
        )
    else:
        per_sequence = gathered_scores(activations, gradients, input_factor, output_factor, lengths)
    blocks = lax.axis_size("layer")
    return layer_sum(per_sequence) / jnp.float32(math.sqrt(RANK * SLOT * blocks))


def solution(mesh):
    in_specs = (
        P("layer", "dp", None),
        P("layer", "dp", None),
        P("layer", "dp", None),
        P("layer", "dp", None),
        P("dp"),
    )
    out_specs = P("dp", None)
    return jax.shard_map(shards, mesh=mesh, in_specs=in_specs, out_specs=out_specs, check_vma=False)
```

```python
import functools
import math

import jax
import jax.numpy as jnp
from jax import lax
from jax.experimental import pallas as pl
from jax.experimental.pallas import tpu as pltpu
from jax.sharding import PartitionSpec as P

RANK = 32
QUERIES = 8
SLOT = 32
STEP = 8
WIDE = 512
MOST = 3
SWAP = [(0, 1), (1, 0)]


def live_tokens(lengths, count):
    position = jnp.arange(count, dtype=jnp.int32)
    sequence = position // SLOT
    owners = sequence[:, None] == jnp.arange(lengths.shape[0], dtype=jnp.int32)[None, :]
    limit = jnp.sum(jnp.where(owners, lengths[None, :], 0), axis=1)
    return (position % SLOT < limit).astype(jnp.float32)


def rank_sum(first, second):
    return jnp.sum((first * second).reshape(first.shape[0], QUERIES, RANK), axis=2)


def gathered_scores(activations, gradients, input_factor, output_factor, lengths):
    tokens = activations.shape[1]
    projected_in = jnp.dot(
        activations[0],
        lax.all_gather(input_factor, "dp", axis=1, tiled=True)[0],
        preferred_element_type=jnp.float32,
    )
    projected_out = jnp.dot(
        gradients[0],
        lax.all_gather(output_factor, "dp", axis=1, tiled=True)[0],
        preferred_element_type=jnp.float32,
    )
    token_score = rank_sum(projected_out, projected_in)
    live = live_tokens(lengths, tokens)
    return jnp.sum(
        (token_score * live[:, None]).reshape(lengths.shape[0], SLOT, QUERIES), axis=1
    )


def selection(lengths_ref, sequences, rows, tokens):
    row = lax.broadcasted_iota(jnp.int32, (rows, tokens), 0)
    slot = lax.broadcasted_iota(jnp.int32, (rows, tokens), 1)
    picked = jnp.zeros((rows, tokens), jnp.bool_)
    before = jnp.int32(0)
    for s in range(sequences):
        length = lengths_ref[s]
        inside = slot - s * SLOT
        picked |= (inside >= 0) & (inside < length) & (row == before + inside)
        before += length
    return jnp.where(picked, 1.0, 0.0).astype(jnp.bfloat16)


VMEM = pl.BlockSpec(memory_space=pltpu.VMEM)
SMEM = pl.BlockSpec(memory_space=pltpu.SMEM)
HBM = pl.BlockSpec(memory_space=pl.ANY)


def limit(mib):
    return pltpu.CompilerParams(vmem_limit_bytes=mib * 1024 * 1024)


def fetch_half(half, ref, buf, sems, parts=2):
    width = buf.shape[1]
    piece = width // parts
    copies = []
    for p in range(parts):
        start = pl.multiple_of(half * width + p * piece, 128)
        copy = pltpu.make_async_copy(
            ref.at[:, pl.ds(start, piece)], buf.at[:, pl.ds(p * piece, piece)], sems.at[p]
        )
        copy.start()
        copies.append((copy, p * piece, piece))
    return copies


def half_scratch(tokens, width):
    return [pltpu.VMEM((tokens, width), jnp.bfloat16), pltpu.SemaphoreType.DMA((2,))]


def pick(select, block):
    return jnp.dot(select, block, preferred_element_type=jnp.float32).astype(jnp.bfloat16)


def first_kernel(total, bounds, lengths_ref, act_ref, out, flags_ref, buf, sems):
    copies = fetch_half(1 - lax.axis_index("dp"), act_ref, buf, sems, 1)
    sequences = lengths_ref.shape[0]
    live = jnp.int32(0)
    for s in range(sequences):
        live += lengths_ref[s]
    most = jnp.maximum(live, total - live)
    which = jnp.int32(0)
    for bound in bounds:
        which += (most > bound).astype(jnp.int32)
    flags_ref[0] = which
    flags_ref[1] = (live > total - live).astype(jnp.int32)
    select = selection(lengths_ref, sequences, out.shape[0], buf.shape[0])
    for copy, start, piece in copies:
        copy.wait()
        out[:, start : start + piece] = pick(select, buf[:, start : start + piece])


def first_rows(total, bounds, lengths, act):
    tokens, width = act.shape[0], act.shape[1] // 2
    return pl.pallas_call(
        functools.partial(first_kernel, total, bounds),
        out_shape=[
            jax.ShapeDtypeStruct((tokens, width), jnp.bfloat16),
            jax.ShapeDtypeStruct((2,), jnp.int32),
        ],
        in_specs=[SMEM, HBM],
        out_specs=[VMEM, SMEM],
        scratch_shapes=half_scratch(tokens, width),
        compiler_params=limit(8),
    )(lengths, act)


def blocks_of(rows, size):
    return [(at, min(size, rows - at)) for at in range(0, rows, size)]


def rest_kernel(chunks, pieces, lent, flags_ref, lengths_ref, act, f_in, grad_ref, *rest):
    outs, (buf, sems, wide) = rest[:-3], rest[-3:]
    copies = fetch_half(1 - lax.axis_index("dp"), grad_ref, buf, sems)
    base, extra, width = sum(chunks), sum(pieces), act.shape[1]
    select = selection(lengths_ref, lengths_ref.shape[0], base + extra, buf.shape[0])
    lender = (flags_ref[1] == 0) & (lent > 0)
    if lent:

        @pl.when(lender)
        def _():
            column = 0
            for at, size in blocks_of(base, extra):
                wide[:size, column : column + lent] = act[at : at + size, :lent]
                column += lent
            for at, size in blocks_of(lent, extra):
                wide[:size, column : column + f_in.shape[1]] = f_in[at : at + size, :]
                column += f_in.shape[1]

    if extra:

        @pl.when(jnp.logical_not(lender))
        def _():
            wide[:, : width - lent] = act[base : base + extra, lent:]

    for copy, start, piece in copies:
        copy.wait()

        def block(i, _, start=start):
            at = pl.multiple_of(start + i * WIDE, WIDE)
            packed = pick(select, buf[:, pl.ds(at, WIDE)])
            row = 0
            for out, size in zip(outs, chunks):
                out[:, pl.ds(at, WIDE)] = packed[row : row + size]
                row += size
            if extra:

                @pl.when(jnp.logical_not(lender))
                def _():
                    wide[:, pl.ds(width - lent + at, WIDE)] = packed[row:]

            return 0

        lax.fori_loop(0, piece // WIDE, block, 0)
    row = 0
    for out, size in zip(outs[len(chunks) :], pieces):
        out[...] = wide[row : row + size, :]
        row += size


def rest_rows(chunks, pieces, lent, flags, lengths, act, f_in, grad):
    tokens, a_wide, g_wide = grad.shape[0], act.shape[1], grad.shape[1] // 2
    shapes = [(n, g_wide) for n in chunks] + [(n, a_wide - lent + g_wide) for n in pieces]
    wide = (sum(pieces), a_wide - lent + g_wide) if pieces else (8, 128)
    return pl.pallas_call(
        functools.partial(rest_kernel, chunks, pieces, lent),
        out_shape=[jax.ShapeDtypeStruct(shape, jnp.bfloat16) for shape in shapes],
        in_specs=[SMEM, SMEM, VMEM, VMEM, HBM],
        out_specs=[VMEM] * len(shapes),
        scratch_shapes=half_scratch(tokens, g_wide) + [pltpu.VMEM(wide, jnp.bfloat16)],
        compiler_params=limit(16),
    )(flags, lengths, act, f_in, grad)


def own_kernel(lengths_ref, act_ref, grad_ref, f_in, f_out, _, out, a_buf, a_sems, g_buf, g_sems):
    half = lax.axis_index("dp")
    sides = (
        (fetch_half(half, act_ref, a_buf, a_sems), a_buf, f_in),
        (fetch_half(half, grad_ref, g_buf, g_sems), g_buf, f_out),
    )
    rows, columns = out.shape[0], f_in.shape[1]
    select = selection(lengths_ref, lengths_ref.shape[0], rows, a_buf.shape[0])
    for side, (copies, buf, factor) in enumerate(sides):
        total = jnp.zeros((rows, columns), jnp.float32)
        for copy, start, piece in copies:
            copy.wait()

            def block(i, total, buf=buf, start=start, factor=factor):
                at = pl.multiple_of(start + i * WIDE, WIDE)
                packed = pick(select, buf[:, pl.ds(at, WIDE)])
                return total + jnp.dot(
                    packed, factor[pl.ds(at, WIDE), :], preferred_element_type=jnp.float32
                )

            total = lax.fori_loop(0, piece // WIDE, block, total)
        out[:, side * columns : (side + 1) * columns] = total


def own_part(rows, lengths, act, grad, f_in, f_out, after, work):
    tokens, columns = act.shape[0], f_in.shape[1]
    return pl.pallas_call(
        own_kernel,
        out_shape=jax.ShapeDtypeStruct((rows, 2 * columns), jnp.float32),
        in_specs=[SMEM, HBM, HBM, VMEM, VMEM, HBM],
        out_specs=VMEM,
        scratch_shapes=half_scratch(tokens, f_in.shape[0]) + half_scratch(tokens, f_out.shape[0]),
        compiler_params=limit(16),
        cost_estimate=pl.CostEstimate(flops=int(work * 1e9), bytes_accessed=0, transcendentals=0)
        if work
        else None,
    )(lengths, act, grad, f_in, f_out, after)


def encode(out, x):
    rows = x.shape[0]
    most = jnp.max(jnp.abs(x), axis=0, keepdims=True)
    power = jnp.ceil(jnp.log2(jnp.maximum(most, 2.0**-100)))
    whole = jnp.clip(jnp.round(x * jnp.exp2(15.0 - power)), -32767.0, 32767.0)
    out[:rows, :] = whole.astype(jnp.int32).astype(jnp.int16)
    out[rows:, :] = jnp.broadcast_to(power, (8, x.shape[1])).astype(jnp.int32).astype(jnp.int16)


def decode(ref, at, size, column, columns):
    rows, span = ref.shape[0] - 8, slice(column, column + columns)
    power = ref[rows : rows + 8, span].astype(jnp.int32).astype(jnp.float32)[:1]
    return ref[at : at + size, span].astype(jnp.int32).astype(jnp.float32) * jnp.exp2(power - 15.0)


def first_project_kernel(lent, x_ref, f_in, out):
    total = jnp.dot(x_ref[...], f_in[lent:, :], preferred_element_type=jnp.float32)
    if lent:
        out[...] = total
    else:
        encode(out, total)


def first_project(lent, x, f_in):
    rows, columns = x.shape[0], f_in.shape[1]
    return pl.pallas_call(
        functools.partial(first_project_kernel, lent),
        out_shape=jax.ShapeDtypeStruct((rows, columns), jnp.float32)
        if lent
        else jax.ShapeDtypeStruct((rows + 8, columns), jnp.int16),
        in_specs=[VMEM] * 2,
        out_specs=VMEM,
        compiler_params=limit(8),
    )(x, f_in)


def project_kernel(x_ref, f_out, out):
    out[...] = jnp.dot(x_ref[...], f_out[...], preferred_element_type=jnp.float32)


def project(x, f_out):
    rows, columns = x.shape[0], f_out.shape[1]
    return pl.pallas_call(
        project_kernel,
        out_shape=jax.ShapeDtypeStruct((rows, columns), jnp.float32),
        in_specs=[VMEM] * 2,
        out_specs=VMEM,
        compiler_params=limit(8),
    )(x, f_out)


def plain_kernel(x_ref, f_in, f_out, out):
    depth = f_in.shape[0]
    inner = jnp.dot(x_ref[:, :depth], f_in[...], preferred_element_type=jnp.float32)
    outer = jnp.dot(x_ref[:, depth:], f_out[...], preferred_element_type=jnp.float32)
    encode(out, jnp.concatenate([inner, outer], axis=1))


def plain_project(x, f_in, f_out):
    return pl.pallas_call(
        plain_kernel,
        out_shape=jax.ShapeDtypeStruct((x.shape[0] + 8, 2 * f_in.shape[1]), jnp.int16),
        in_specs=[VMEM] * 3,
        out_specs=VMEM,
        compiler_params=limit(8),
    )(x, f_in, f_out)


def extra_kernel(lent, base, flags_ref, made, act, f_in, f_out, *rest):
    pieces, (back, added, total, a_buf, f_buf, x_ref) = rest[:-6], rest[-6:]
    extra, (width, columns) = x_ref.shape[0], f_in.shape
    rows = base + extra
    row = 0
    for piece in pieces:
        x_ref[row : row + piece.shape[0], :] = piece[...]
        row += piece.shape[0]
    borrower = flags_ref[1] == 1

    @pl.when(borrower)
    def _():
        column = 0
        for at, size in blocks_of(base, extra):
            a_buf[at : at + size, :] = x_ref[:size, column : column + lent]
            column += lent
        for at, size in blocks_of(lent, extra):
            f_buf[at : at + size, :] = x_ref[:size, column : column + columns]
            column += columns
        total[:base, :] = made[...] + jnp.dot(
            a_buf[...], f_in[:lent, :], preferred_element_type=jnp.float32
        )
        total[base:, :] = jnp.zeros((2 * extra, columns), jnp.float32)
        added[...] = jnp.dot(act[:rows, :lent], f_buf[...], preferred_element_type=jnp.float32)

    @pl.when(jnp.logical_not(borrower))
    def _():
        total[:base, :] = made[...]
        total[base:rows, :] = jnp.dot(
            x_ref[:, : width - lent], f_in[lent:, :], preferred_element_type=jnp.float32
        )
        total[rows:, :] = jnp.dot(
            x_ref[:, width - lent :], f_out[...], preferred_element_type=jnp.float32
        )
        added[...] = jnp.zeros((rows, columns), jnp.float32)

    encode(back, total[...])


def extra_rows(lent, flags, made, pieces, act, f_in, f_out):
    base, extra, columns = made.shape[0], sum(x.shape[0] for x in pieces), f_in.shape[1]
    return pl.pallas_call(
        functools.partial(extra_kernel, lent, base),
        out_shape=[
            jax.ShapeDtypeStruct((base + 2 * extra + 8, columns), jnp.int16),
            jax.ShapeDtypeStruct((base + extra, columns), jnp.float32),
        ],
        in_specs=[SMEM] + [VMEM] * (4 + len(pieces)),
        out_specs=[VMEM, VMEM],
        scratch_shapes=[
            pltpu.VMEM((base + 2 * extra, columns), jnp.float32),
            pltpu.VMEM((base, lent), jnp.bfloat16),
            pltpu.VMEM((lent, columns), jnp.bfloat16),
            pltpu.VMEM((extra, pieces[0].shape[1]), jnp.bfloat16),
        ],
        compiler_params=limit(8),
    )(flags, made, act, f_in, f_out, *pieces)


def score_kernel(spans, lengths_ref, *rest):
    arrays, out_ref = rest[:-1], rest[-1]
    columns, sequences = QUERIES * RANK, lengths_ref.shape[0]
    sums = [jnp.zeros((1, columns), jnp.float32) for _ in range(sequences)]
    for first, size, sides in spans:
        total = [
            sum(
                decode(arrays[which], at, size, column, columns)
                if arrays[which].dtype == jnp.int16
                else arrays[which][at : at + size, column : column + columns]
                for which, at, column in parts
            )
            for parts in sides
        ]
        product = total[0] * total[1]
        row = first + lax.broadcasted_iota(jnp.int32, (size, columns), 0)
        before = jnp.int32(0)
        for s in range(sequences):
            after = before + lengths_ref[s]
            mine = (row >= before) & (row < after)
            sums[s] += jnp.sum(jnp.where(mine, product, 0.0), axis=0, keepdims=True)
            before = after
    total = jnp.concatenate(sums, axis=0)
    out_ref[...] = jnp.concatenate(
        [jnp.sum(total[:, q * RANK : (q + 1) * RANK], axis=1, keepdims=True) for q in range(QUERIES)],
        axis=1,
    )


def score(spans, lengths, arrays):
    return pl.pallas_call(
        functools.partial(score_kernel, spans),
        out_shape=jax.ShapeDtypeStruct((lengths.shape[0], QUERIES), jnp.float32),
        in_specs=[SMEM] + [VMEM] * len(arrays),
        out_specs=VMEM,
        compiler_params=limit(4),
    )(lengths, *arrays)


def lendable(base, extra, columns, a_wide, g_wide):
    best = 0
    for lent in range(128, a_wide, 128):
        used = len(blocks_of(base, extra)) * lent + len(blocks_of(lent, extra)) * columns
        if used <= a_wide - lent + g_wide:
            best = lent
    return best


def swap(x):
    return lax.ppermute(x, "dp", SWAP)


def swapped_scores(rows, base, lent, chunks, flags, lengths, packed, act, grad, f_in, f_out):
    columns, extra = f_in.shape[1], rows - base
    first = swap(packed[:base, lent:])
    sent = rest_rows(chunks, [extra], lent, flags, lengths, packed, f_in, grad)
    groups = list(zip(sent, [sum(chunks[:i]) for i in range(len(chunks))] + [base]))
    groups.sort(key=lambda group: -group[0].size)
    arrived = [swap(x) for x, _ in groups]
    if lent:
        made = first_project(lent, first, f_in)
        done = own = own_part(rows, lengths, act, grad, f_in, f_out, made, 1.7 if extra <= 3 * STEP else 2.9)
    else:
        own = own_part(rows, lengths, act, grad, f_in, f_out, lengths, 0)
        first, own = lax.optimization_barrier((first, own))
        done = made = first_project(lent, first, f_in)
    arrays, spans, in_parts = [own], [], [0]
    if not lent:
        in_parts.append(len(arrays))
        arrays.append(swap(made))
    for x, (_, at) in zip(arrived, groups):
        x, done = lax.optimization_barrier((x, done))
        here = len(arrays)
        if at < base:
            done = project(x, f_out)
            spans.append((at, x.shape[0], (here, 0, 0)))
        elif not lent:
            done = plain_project(x, f_in, f_out)
            spans.append((at, extra, (here, 0, columns)))
        else:
            done, added = extra_rows(lent, flags, made, [x], packed, f_in, f_out)
            in_parts += [here, here + 1]
            spans.append((at, extra, (here, rows, 0)))
        arrays.append(swap(done))
        if lent and at == base:
            arrays.append(added)
    spans = [
        (
            at,
            size,
            (
                ((0, at, 0), (back[0], 0, 0))
                if at == base and not lent
                else tuple((which, at, 0) for which in in_parts),
                ((0, at, columns), back),
            ),
        )
        for at, size, back in spans
    ]
    return score(spans, lengths, arrays)


def plan(rows, even, a_wide, g_wide, columns):
    if rows <= even + STEP:
        base = even - STEP
        large = (base + STEP) // 2 // STEP * STEP
        return rows, base, 0, [large, base - large]
    base = even - STEP
    large = (base // 2) // STEP * STEP
    lent = lendable(base, rows - base, columns, a_wide, g_wide)
    return rows, base, lent, [large, base - STEP - large, STEP]


def layer_sum(x):
    size = lax.axis_size("layer")
    if size & (size - 1):
        return lax.psum(x, "layer")
    bits = [1 << i for i in range(size.bit_length() - 1)]
    steps = [bits[:1], bits[1:3], *([b] for b in bits[3:])]
    for step in steps:
        flips = [0]
        for bit in step:
            flips += [flip ^ bit for flip in flips]
        x = sum((lax.ppermute(x, "layer", [(i, i ^ flip) for i in range(size)]) for flip in flips[1:]), x)
    return x


def shards(activations, gradients, input_factor, output_factor, lengths):
    tokens = activations.shape[1]
    parts = lax.axis_size("dp")
    widths = (input_factor.shape[1], output_factor.shape[1])
    if parts == 2 and all(w % (2 * WIDE) == 0 for w in widths):
        act, grad, f_in, f_out = (x[0] for x in (activations, gradients, input_factor, output_factor))
        total = 5 * parts * tokens // 8
        even = (total // 2 + STEP - 1) // STEP * STEP
        sizes = [n for n in range(even, tokens, STEP) if n <= even + MOST * STEP] + [tokens]
        bounds = sizes[:-1]
        packed, flags = first_rows(total, bounds, lengths, act)
        plans = [plan(rows, even, *widths, f_in.shape[1]) for rows in sizes]
        per_sequence = lax.switch(
            flags[0],
            [functools.partial(swapped_scores, *p) for p in plans],
            *(flags, lengths, packed, act, grad, f_in, f_out),
        )
    else:
        per_sequence = gathered_scores(activations, gradients, input_factor, output_factor, lengths)
    blocks = lax.axis_size("layer")
    return layer_sum(per_sequence) / jnp.float32(math.sqrt(RANK * SLOT * blocks))


def solution(mesh):
    in_specs = (
        P("layer", "dp", None),
        P("layer", "dp", None),
        P("layer", "dp", None),
        P("layer", "dp", None),
        P("dp"),
    )
    out_specs = P("dp", None)
    return jax.shard_map(shards, mesh=mesh, in_specs=in_specs, out_specs=out_specs, check_vma=False)
```

```python
import functools
import math

import jax
import jax.numpy as jnp
from jax import lax
from jax.experimental import pallas as pl
from jax.experimental.pallas import tpu as pltpu
from jax.sharding import PartitionSpec as P

RANK = 32
QUERIES = 8
SLOT = 32
STEP = 8
WIDE = 512
MOST = 3
LEAD = 2048
SWAP = [(0, 1), (1, 0)]


def live_tokens(lengths, count):
    position = jnp.arange(count, dtype=jnp.int32)
    sequence = position // SLOT
    owners = sequence[:, None] == jnp.arange(lengths.shape[0], dtype=jnp.int32)[None, :]
    limit = jnp.sum(jnp.where(owners, lengths[None, :], 0), axis=1)
    return (position % SLOT < limit).astype(jnp.float32)


def rank_sum(first, second):
    return jnp.sum((first * second).reshape(first.shape[0], QUERIES, RANK), axis=2)


def gathered_scores(activations, gradients, input_factor, output_factor, lengths):
    tokens = activations.shape[1]
    projected_in = jnp.dot(
        activations[0],
        lax.all_gather(input_factor, "dp", axis=1, tiled=True)[0],
        preferred_element_type=jnp.float32,
    )
    projected_out = jnp.dot(
        gradients[0],
        lax.all_gather(output_factor, "dp", axis=1, tiled=True)[0],
        preferred_element_type=jnp.float32,
    )
    token_score = rank_sum(projected_out, projected_in)
    live = live_tokens(lengths, tokens)
    return jnp.sum(
        (token_score * live[:, None]).reshape(lengths.shape[0], SLOT, QUERIES), axis=1
    )


def selection(lengths_ref, sequences, rows, tokens):
    row = lax.broadcasted_iota(jnp.int32, (rows, tokens), 0)
    slot = lax.broadcasted_iota(jnp.int32, (rows, tokens), 1)
    picked = jnp.zeros((rows, tokens), jnp.bool_)
    before = jnp.int32(0)
    for s in range(sequences):
        length = lengths_ref[s]
        inside = slot - s * SLOT
        picked |= (inside >= 0) & (inside < length) & (row == before + inside)
        before += length
    return jnp.where(picked, 1.0, 0.0).astype(jnp.bfloat16)


VMEM = pl.BlockSpec(memory_space=pltpu.VMEM)
SMEM = pl.BlockSpec(memory_space=pltpu.SMEM)
HBM = pl.BlockSpec(memory_space=pl.ANY)


def limit(mib):
    return pltpu.CompilerParams(vmem_limit_bytes=mib * 1024 * 1024)


def fetch_half(half, ref, buf, sems, parts=2):
    width = buf.shape[1]
    piece = width // parts
    copies = []
    for p in range(parts):
        start = pl.multiple_of(half * width + p * piece, 128)
        copy = pltpu.make_async_copy(
            ref.at[:, pl.ds(start, piece)], buf.at[:, pl.ds(p * piece, piece)], sems.at[p]
        )
        copy.start()
        copies.append((copy, p * piece, piece))
    return copies


def half_scratch(tokens, width):
    return [pltpu.VMEM((tokens, width), jnp.bfloat16), pltpu.SemaphoreType.DMA((2,))]


def pick(select, block):
    return jnp.dot(select, block, preferred_element_type=jnp.float32).astype(jnp.bfloat16)


def first_kernel(total, bounds, lengths_ref, act_ref, out, flags_ref, buf, sems):
    copies = fetch_half(1 - lax.axis_index("dp"), act_ref, buf, sems, 1)
    sequences = lengths_ref.shape[0]
    live = jnp.int32(0)
    for s in range(sequences):
        live += lengths_ref[s]
    most = jnp.maximum(live, total - live)
    which = jnp.int32(0)
    for bound in bounds:
        which += (most > bound).astype(jnp.int32)
    flags_ref[0] = which
    flags_ref[1] = (live > total - live).astype(jnp.int32)
    select = selection(lengths_ref, sequences, out.shape[0], buf.shape[0])
    for copy, start, piece in copies:
        copy.wait()
        out[:, start : start + piece] = pick(select, buf[:, start : start + piece])


def first_rows(total, bounds, lengths, act):
    tokens, width = act.shape[0], act.shape[1] // 2
    return pl.pallas_call(
        functools.partial(first_kernel, total, bounds),
        out_shape=[
            jax.ShapeDtypeStruct((tokens, width), jnp.bfloat16),
            jax.ShapeDtypeStruct((2,), jnp.int32),
        ],
        in_specs=[SMEM, HBM],
        out_specs=[VMEM, SMEM],
        scratch_shapes=half_scratch(tokens, width),
        compiler_params=limit(8),
    )(lengths, act)


def blocks_of(rows, size):
    return [(at, min(size, rows - at)) for at in range(0, rows, size)]


def rest_kernel(chunks, extra, cuts, lent, flags_ref, lengths_ref, act, f_in, grad_ref, *rest):
    outs, (buf, sems, wide) = rest[:-3], rest[-3:]
    copies = fetch_half(1 - lax.axis_index("dp"), grad_ref, buf, sems)
    base, width = sum(chunks), act.shape[1]
    select = selection(lengths_ref, lengths_ref.shape[0], base + extra, buf.shape[0])
    lender = (flags_ref[1] == 0) & (lent > 0)
    if lent:

        @pl.when(lender)
        def _():
            column = 0
            for at, size in blocks_of(base, extra):
                wide[:size, column : column + lent] = act[at : at + size, :lent]
                column += lent
            for at, size in blocks_of(lent, extra):
                wide[:size, column : column + f_in.shape[1]] = f_in[at : at + size, :]
                column += f_in.shape[1]

    if extra:

        @pl.when(jnp.logical_not(lender))
        def _():
            wide[:, : width - lent] = act[base : base + extra, lent:]

    for copy, start, piece in copies:
        copy.wait()

        def block(i, _, start=start):
            at = pl.multiple_of(start + i * WIDE, WIDE)
            packed = pick(select, buf[:, pl.ds(at, WIDE)])
            row = 0
            for out, size in zip(outs, chunks):
                out[:, pl.ds(at, WIDE)] = packed[row : row + size]
                row += size
            if extra:

                @pl.when(jnp.logical_not(lender))
                def _():
                    wide[:, pl.ds(width - lent + at, WIDE)] = packed[row:]

            return 0

        lax.fori_loop(0, piece // WIDE, block, 0)
    column = 0
    for out, size in zip(outs[len(chunks) :], cuts):
        out[...] = wide[:, column : column + size]
        column += size


def rest_rows(chunks, extra, cuts, lent, flags, lengths, act, f_in, grad):
    tokens, a_wide, g_wide = grad.shape[0], act.shape[1], grad.shape[1] // 2
    shapes = [(n, g_wide) for n in chunks] + [(extra, n) for n in cuts]
    return pl.pallas_call(
        functools.partial(rest_kernel, chunks, extra, cuts, lent),
        out_shape=[jax.ShapeDtypeStruct(shape, jnp.bfloat16) for shape in shapes],
        in_specs=[SMEM, SMEM, VMEM, VMEM, HBM],
        out_specs=[VMEM] * len(shapes),
        scratch_shapes=half_scratch(tokens, g_wide) + [pltpu.VMEM((extra, sum(cuts)), jnp.bfloat16)],
        compiler_params=limit(16),
    )(flags, lengths, act, f_in, grad)


def own_kernel(lengths_ref, act_ref, grad_ref, f_in, f_out, _, out, a_buf, a_sems, g_buf, g_sems):
    half = lax.axis_index("dp")
    sides = (
        (fetch_half(half, act_ref, a_buf, a_sems), a_buf, f_in),
        (fetch_half(half, grad_ref, g_buf, g_sems), g_buf, f_out),
    )
    rows, columns = out.shape[0], f_in.shape[1]
    select = selection(lengths_ref, lengths_ref.shape[0], rows, a_buf.shape[0])
    for side, (copies, buf, factor) in enumerate(sides):
        total = jnp.zeros((rows, columns), jnp.float32)
        for copy, start, piece in copies:
            copy.wait()

            def block(i, total, buf=buf, start=start, factor=factor):
                at = pl.multiple_of(start + i * WIDE, WIDE)
                packed = pick(select, buf[:, pl.ds(at, WIDE)])
                return total + jnp.dot(
                    packed, factor[pl.ds(at, WIDE), :], preferred_element_type=jnp.float32
                )

            total = lax.fori_loop(0, piece // WIDE, block, total)
        out[:, side * columns : (side + 1) * columns] = total


def own_part(rows, lengths, act, grad, f_in, f_out, after, work):
    tokens, columns = act.shape[0], f_in.shape[1]
    return pl.pallas_call(
        own_kernel,
        out_shape=jax.ShapeDtypeStruct((rows, 2 * columns), jnp.float32),
        in_specs=[SMEM, HBM, HBM, VMEM, VMEM, HBM],
        out_specs=VMEM,
        scratch_shapes=half_scratch(tokens, f_in.shape[0]) + half_scratch(tokens, f_out.shape[0]),
        compiler_params=limit(16),
        cost_estimate=pl.CostEstimate(flops=int(work * 1e9), bytes_accessed=0, transcendentals=0)
        if work
        else None,
    )(lengths, act, grad, f_in, f_out, after)


def encode(out, x):
    rows = x.shape[0]
    most = jnp.max(jnp.abs(x), axis=0, keepdims=True)
    power = jnp.ceil(jnp.log2(jnp.maximum(most, 2.0**-100)) + 0.01)
    whole = jnp.clip(jnp.round(x * jnp.exp2(15.0 - power)), -32767.0, 32767.0)
    out[:rows, :] = whole.astype(jnp.int32).astype(jnp.int16)
    out[rows:, :] = jnp.broadcast_to(power, (8, x.shape[1])).astype(jnp.int32).astype(jnp.int16)


def decode(ref, at, size, column, columns):
    rows, span = ref.shape[0] - 8, slice(column, column + columns)
    power = ref[rows : rows + 8, span].astype(jnp.int32).astype(jnp.float32)[:1]
    return ref[at : at + size, span].astype(jnp.int32).astype(jnp.float32) * jnp.exp2(power - 15.0)


def first_project_kernel(lent, x_ref, f_in, out):
    total = jnp.dot(x_ref[...], f_in[lent:, :], preferred_element_type=jnp.float32)
    if lent:
        out[...] = total
    else:
        encode(out, total)


def first_project(lent, x, f_in):
    rows, columns = x.shape[0], f_in.shape[1]
    return pl.pallas_call(
        functools.partial(first_project_kernel, lent),
        out_shape=jax.ShapeDtypeStruct((rows, columns), jnp.float32)
        if lent
        else jax.ShapeDtypeStruct((rows + 8, columns), jnp.int16),
        in_specs=[VMEM] * 2,
        out_specs=VMEM,
        compiler_params=limit(8),
    )(x, f_in)


def project_kernel(x_ref, f_out, out):
    out[...] = jnp.dot(x_ref[...], f_out[...], preferred_element_type=jnp.float32)


def project(x, f_out):
    rows, columns = x.shape[0], f_out.shape[1]
    return pl.pallas_call(
        project_kernel,
        out_shape=jax.ShapeDtypeStruct((rows, columns), jnp.float32),
        in_specs=[VMEM] * 2,
        out_specs=VMEM,
        compiler_params=limit(8),
    )(x, f_out)


def begin_kernel(x_ref, f_in, f_out, out):
    depth, columns = f_in.shape
    out[:, :columns] = jnp.dot(x_ref[:, :depth], f_in[...], preferred_element_type=jnp.float32)
    out[:, columns:] = jnp.dot(
        x_ref[:, depth:], f_out[: x_ref.shape[1] - depth, :], preferred_element_type=jnp.float32
    )


def begin(x, f_in, f_out):
    return pl.pallas_call(
        begin_kernel,
        out_shape=jax.ShapeDtypeStruct((x.shape[0], 2 * f_in.shape[1]), jnp.float32),
        in_specs=[VMEM] * 3,
        out_specs=VMEM,
        compiler_params=limit(8),
    )(x, f_in, f_out)


def finish_kernel(x_ref, made, f_out, out):
    depth, columns = f_out.shape
    outer = made[:, columns:] + jnp.dot(
        x_ref[...], f_out[depth - x_ref.shape[1] :, :], preferred_element_type=jnp.float32
    )
    encode(out, jnp.concatenate([made[:, :columns], outer], axis=1))


def finish(x, made, f_out):
    return pl.pallas_call(
        finish_kernel,
        out_shape=jax.ShapeDtypeStruct((x.shape[0] + 8, made.shape[1]), jnp.int16),
        in_specs=[VMEM] * 3,
        out_specs=VMEM,
        compiler_params=limit(8),
    )(x, made, f_out)


def extra_kernel(lent, base, flags_ref, made, act, f_in, f_out, *rest):
    pieces, (back, added, total, a_buf, f_buf, x_ref) = rest[:-6], rest[-6:]
    extra, (width, columns) = x_ref.shape[0], f_in.shape
    rows = base + extra
    row = 0
    for piece in pieces:
        x_ref[row : row + piece.shape[0], :] = piece[...]
        row += piece.shape[0]
    borrower = flags_ref[1] == 1

    @pl.when(borrower)
    def _():
        column = 0
        for at, size in blocks_of(base, extra):
            a_buf[at : at + size, :] = x_ref[:size, column : column + lent]
            column += lent
        for at, size in blocks_of(lent, extra):
            f_buf[at : at + size, :] = x_ref[:size, column : column + columns]
            column += columns
        total[:base, :] = made[...] + jnp.dot(
            a_buf[...], f_in[:lent, :], preferred_element_type=jnp.float32
        )
        total[base:, :] = jnp.zeros((2 * extra, columns), jnp.float32)
        added[...] = jnp.dot(act[:rows, :lent], f_buf[...], preferred_element_type=jnp.float32)

    @pl.when(jnp.logical_not(borrower))
    def _():
        total[:base, :] = made[...]
        total[base:rows, :] = jnp.dot(
            x_ref[:, : width - lent], f_in[lent:, :], preferred_element_type=jnp.float32
        )
        total[rows:, :] = jnp.dot(
            x_ref[:, width - lent :], f_out[...], preferred_element_type=jnp.float32
        )
        added[...] = jnp.zeros((rows, columns), jnp.float32)

    encode(back, total[...])


def extra_rows(lent, flags, made, pieces, act, f_in, f_out):
    base, extra, columns = made.shape[0], sum(x.shape[0] for x in pieces), f_in.shape[1]
    return pl.pallas_call(
        functools.partial(extra_kernel, lent, base),
        out_shape=[
            jax.ShapeDtypeStruct((base + 2 * extra + 8, columns), jnp.int16),
            jax.ShapeDtypeStruct((base + extra, columns), jnp.float32),
        ],
        in_specs=[SMEM] + [VMEM] * (4 + len(pieces)),
        out_specs=[VMEM, VMEM],
        scratch_shapes=[
            pltpu.VMEM((base + 2 * extra, columns), jnp.float32),
            pltpu.VMEM((base, lent), jnp.bfloat16),
            pltpu.VMEM((lent, columns), jnp.bfloat16),
            pltpu.VMEM((extra, pieces[0].shape[1]), jnp.bfloat16),
        ],
        compiler_params=limit(8),
    )(flags, made, act, f_in, f_out, *pieces)


def score_kernel(spans, lengths_ref, *rest):
    arrays, out_ref = rest[:-1], rest[-1]
    columns, sequences = QUERIES * RANK, lengths_ref.shape[0]
    sums = [jnp.zeros((1, columns), jnp.float32) for _ in range(sequences)]
    for first, size, sides in spans:
        total = [
            sum(
                decode(arrays[which], at, size, column, columns)
                if arrays[which].dtype == jnp.int16
                else arrays[which][at : at + size, column : column + columns]
                for which, at, column in parts
            )
            for parts in sides
        ]
        product = total[0] * total[1]
        row = first + lax.broadcasted_iota(jnp.int32, (size, columns), 0)
        before = jnp.int32(0)
        for s in range(sequences):
            after = before + lengths_ref[s]
            mine = (row >= before) & (row < after)
            sums[s] += jnp.sum(jnp.where(mine, product, 0.0), axis=0, keepdims=True)
            before = after
    total = jnp.concatenate(sums, axis=0)
    out_ref[...] = jnp.concatenate(
        [jnp.sum(total[:, q * RANK : (q + 1) * RANK], axis=1, keepdims=True) for q in range(QUERIES)],
        axis=1,
    )


def score(spans, lengths, arrays):
    return pl.pallas_call(
        functools.partial(score_kernel, spans),
        out_shape=jax.ShapeDtypeStruct((lengths.shape[0], QUERIES), jnp.float32),
        in_specs=[SMEM] + [VMEM] * len(arrays),
        out_specs=VMEM,
        compiler_params=limit(4),
    )(lengths, *arrays)


def lendable(base, extra, columns, a_wide, g_wide):
    best = 0
    for lent in range(128, a_wide, 128):
        used = len(blocks_of(base, extra)) * lent + len(blocks_of(lent, extra)) * columns
        if used <= a_wide - lent + g_wide:
            best = lent
    return best


def swap(x):
    return lax.ppermute(x, "dp", SWAP)


def swapped_scores(rows, base, lent, chunks, flags, lengths, packed, act, grad, f_in, f_out):
    columns, extra = f_in.shape[1], rows - base
    first = swap(packed[:base, lent:])
    width = f_in.shape[0] - lent + f_out.shape[0]
    cuts = [width] if lent else [f_in.shape[0] + LEAD, f_out.shape[0] - LEAD]
    sent = rest_rows(chunks, extra, cuts, lent, flags, lengths, packed, f_in, grad)
    groups = list(zip(sent, [sum(chunks[:i]) for i in range(len(chunks))] + [base] * len(cuts)))
    groups.sort(key=lambda group: -group[0].size)
    arrived = [swap(x) for x, _ in groups]
    if lent:
        made = first_project(lent, first, f_in)
        done = own = own_part(rows, lengths, act, grad, f_in, f_out, made, 1.7 if extra <= 3 * STEP else 2.9)
    else:
        own = own_part(rows, lengths, act, grad, f_in, f_out, lengths, 0)
        first, own = lax.optimization_barrier((first, own))
        done = made = first_project(lent, first, f_in)
    arrays, spans, in_parts = [own], [], [0]
    if not lent:
        in_parts.append(len(arrays))
        arrays.append(swap(made))
    for x, (_, at) in zip(arrived, groups):
        x, done = lax.optimization_barrier((x, done))
        here = len(arrays)
        if at < base:
            done = project(x, f_out)
            spans.append((at, x.shape[0], (here, 0, 0)))
        elif not lent and x.shape[1] == cuts[0]:
            done = begun = begin(x, f_in, f_out)
            continue
        elif not lent:
            done = finish(x, begun, f_out)
            spans.append((at, extra, (here, 0, columns)))
        else:
            done, added = extra_rows(lent, flags, made, [x], packed, f_in, f_out)
            in_parts += [here, here + 1]
            spans.append((at, extra, (here, rows, 0)))
        arrays.append(swap(done))
        if lent and at == base:
            arrays.append(added)
    spans = [
        (
            at,
            size,
            (
                ((0, at, 0), (back[0], 0, 0))
                if at == base and not lent
                else tuple((which, at, 0) for which in in_parts),
                ((0, at, columns), back),
            ),
        )
        for at, size, back in spans
    ]
    return score(spans, lengths, arrays)


def plan(rows, even, a_wide, g_wide, columns):
    if rows <= even + STEP:
        base = even - STEP
        large = (base + STEP) // 2 // STEP * STEP
        return rows, base, 0, [large, base - large]
    base = even - STEP
    large = (base // 2) // STEP * STEP
    lent = lendable(base, rows - base, columns, a_wide, g_wide)
    return rows, base, lent, [large, base - STEP - large, STEP]


def layer_sum(x):
    size = lax.axis_size("layer")
    if size & (size - 1):
        return lax.psum(x, "layer")
    bits = [1 << i for i in range(size.bit_length() - 1)]
    steps = [bits[:1], bits[1:3], *([b] for b in bits[3:])]
    for step in steps:
        flips = [0]
        for bit in step:
            flips += [flip ^ bit for flip in flips]
        x = sum((lax.ppermute(x, "layer", [(i, i ^ flip) for i in range(size)]) for flip in flips[1:]), x)
    return x


def shards(activations, gradients, input_factor, output_factor, lengths):
    tokens = activations.shape[1]
    parts = lax.axis_size("dp")
    widths = (input_factor.shape[1], output_factor.shape[1])
    if parts == 2 and all(w % (2 * WIDE) == 0 for w in widths) and widths[1] > 2 * LEAD:
        act, grad, f_in, f_out = (x[0] for x in (activations, gradients, input_factor, output_factor))
        total = 5 * parts * tokens // 8
        even = (total // 2 + STEP - 1) // STEP * STEP
        sizes = [n for n in range(even, tokens, STEP) if n <= even + MOST * STEP] + [tokens]
        bounds = sizes[:-1]
        packed, flags = first_rows(total, bounds, lengths, act)
        plans = [plan(rows, even, *widths, f_in.shape[1]) for rows in sizes]
        per_sequence = lax.switch(
            flags[0],
            [functools.partial(swapped_scores, *p) for p in plans],
            *(flags, lengths, packed, act, grad, f_in, f_out),
        )
    else:
        per_sequence = gathered_scores(activations, gradients, input_factor, output_factor, lengths)
    blocks = lax.axis_size("layer")
    return layer_sum(per_sequence) / jnp.float32(math.sqrt(RANK * SLOT * blocks))


def solution(mesh):
    in_specs = (
        P("layer", "dp", None),
        P("layer", "dp", None),
        P("layer", "dp", None),
        P("layer", "dp", None),
        P("dp"),
    )
    out_specs = P("dp", None)
    return jax.shard_map(shards, mesh=mesh, in_specs=in_specs, out_specs=out_specs, check_vma=False)
```

```python
import functools
import math

import jax
import jax.numpy as jnp
from jax import lax
from jax.experimental import pallas as pl
from jax.experimental.pallas import tpu as pltpu
from jax.sharding import PartitionSpec as P

RANK = 32
QUERIES = 8
SLOT = 32
STEP = 8
WIDE = 512
MOST = 3
LEAD = 2048
SWAP = [(0, 1), (1, 0)]


def live_tokens(lengths, count):
    position = jnp.arange(count, dtype=jnp.int32)
    sequence = position // SLOT
    owners = sequence[:, None] == jnp.arange(lengths.shape[0], dtype=jnp.int32)[None, :]
    limit = jnp.sum(jnp.where(owners, lengths[None, :], 0), axis=1)
    return (position % SLOT < limit).astype(jnp.float32)


def rank_sum(first, second):
    return jnp.sum((first * second).reshape(first.shape[0], QUERIES, RANK), axis=2)


def gathered_scores(activations, gradients, input_factor, output_factor, lengths):
    tokens = activations.shape[1]
    projected_in = jnp.dot(
        activations[0],
        lax.all_gather(input_factor, "dp", axis=1, tiled=True)[0],
        preferred_element_type=jnp.float32,
    )
    projected_out = jnp.dot(
        gradients[0],
        lax.all_gather(output_factor, "dp", axis=1, tiled=True)[0],
        preferred_element_type=jnp.float32,
    )
    token_score = rank_sum(projected_out, projected_in)
    live = live_tokens(lengths, tokens)
    return jnp.sum(
        (token_score * live[:, None]).reshape(lengths.shape[0], SLOT, QUERIES), axis=1
    )


def selection(lengths_ref, sequences, rows, tokens):
    row = lax.broadcasted_iota(jnp.int32, (rows, tokens), 0)
    slot = lax.broadcasted_iota(jnp.int32, (rows, tokens), 1)
    picked = jnp.zeros((rows, tokens), jnp.bool_)
    before = jnp.int32(0)
    for s in range(sequences):
        length = lengths_ref[s]
        inside = slot - s * SLOT
        picked |= (inside >= 0) & (inside < length) & (row == before + inside)
        before += length
    return jnp.where(picked, 1.0, 0.0).astype(jnp.bfloat16)


VMEM = pl.BlockSpec(memory_space=pltpu.VMEM)
SMEM = pl.BlockSpec(memory_space=pltpu.SMEM)
HBM = pl.BlockSpec(memory_space=pl.ANY)


def limit(mib):
    return pltpu.CompilerParams(vmem_limit_bytes=mib * 1024 * 1024)


def fetch_half(half, ref, buf, sems, parts=2):
    width = buf.shape[1]
    piece = width // parts
    copies = []
    for p in range(parts):
        start = pl.multiple_of(half * width + p * piece, 128)
        copy = pltpu.make_async_copy(
            ref.at[:, pl.ds(start, piece)], buf.at[:, pl.ds(p * piece, piece)], sems.at[p]
        )
        copy.start()
        copies.append((copy, p * piece, piece))
    return copies


def half_scratch(tokens, width):
    return [pltpu.VMEM((tokens, width), jnp.bfloat16), pltpu.SemaphoreType.DMA((2,))]


def pick(select, block):
    return jnp.dot(select, block, preferred_element_type=jnp.float32).astype(jnp.bfloat16)


def first_kernel(total, bounds, lengths_ref, act_ref, out, flags_ref, buf, sems):
    copies = fetch_half(1 - lax.axis_index("dp"), act_ref, buf, sems, 1)
    sequences = lengths_ref.shape[0]
    live = jnp.int32(0)
    for s in range(sequences):
        live += lengths_ref[s]
    most = jnp.maximum(live, total - live)
    which = jnp.int32(0)
    for bound in bounds:
        which += (most > bound).astype(jnp.int32)
    flags_ref[0] = which
    flags_ref[1] = (live > total - live).astype(jnp.int32)
    select = selection(lengths_ref, sequences, out.shape[0], buf.shape[0])
    for copy, start, piece in copies:
        copy.wait()
        out[:, start : start + piece] = pick(select, buf[:, start : start + piece])


def first_rows(total, bounds, lengths, act):
    tokens, width = act.shape[0], act.shape[1] // 2
    return pl.pallas_call(
        functools.partial(first_kernel, total, bounds),
        out_shape=[
            jax.ShapeDtypeStruct((tokens, width), jnp.bfloat16),
            jax.ShapeDtypeStruct((2,), jnp.int32),
        ],
        in_specs=[SMEM, HBM],
        out_specs=[VMEM, SMEM],
        scratch_shapes=half_scratch(tokens, width),
        compiler_params=limit(8),
    )(lengths, act)


def blocks_of(rows, size):
    return [(at, min(size, rows - at)) for at in range(0, rows, size)]


def rest_kernel(chunks, extra, cuts, lent, flags_ref, lengths_ref, act, f_in, grad_ref, *rest):
    outs, (buf, sems, wide) = rest[:-3], rest[-3:]
    copies = fetch_half(1 - lax.axis_index("dp"), grad_ref, buf, sems)
    base, width = sum(chunks), act.shape[1]
    select = selection(lengths_ref, lengths_ref.shape[0], base + extra, buf.shape[0])
    lender = (flags_ref[1] == 0) & (lent > 0)
    if lent:

        @pl.when(lender)
        def _():
            column = 0
            for at, size in blocks_of(base, extra):
                wide[:size, column : column + lent] = act[at : at + size, :lent]
                column += lent
            for at, size in blocks_of(lent, extra):
                wide[:size, column : column + f_in.shape[1]] = f_in[at : at + size, :]
                column += f_in.shape[1]

    if extra:

        @pl.when(jnp.logical_not(lender))
        def _():
            wide[:, : width - lent] = act[base : base + extra, lent:]

    for copy, start, piece in copies:
        copy.wait()

        def block(i, _, start=start):
            at = pl.multiple_of(start + i * WIDE, WIDE)
            packed = pick(select, buf[:, pl.ds(at, WIDE)])
            row = 0
            for out, size in zip(outs, chunks):
                out[:, pl.ds(at, WIDE)] = packed[row : row + size]
                row += size
            if extra:

                @pl.when(jnp.logical_not(lender))
                def _():
                    wide[:, pl.ds(width - lent + at, WIDE)] = packed[row:]

            return 0

        lax.fori_loop(0, piece // WIDE, block, 0)
    column = 0
    for out, size in zip(outs[len(chunks) :], cuts):
        out[...] = wide[:, column : column + size]
        column += size


def rest_rows(chunks, extra, cuts, lent, flags, lengths, act, f_in, grad):
    tokens, a_wide, g_wide = grad.shape[0], act.shape[1], grad.shape[1] // 2
    shapes = [(n, g_wide) for n in chunks] + [(extra, n) for n in cuts]
    return pl.pallas_call(
        functools.partial(rest_kernel, chunks, extra, cuts, lent),
        out_shape=[jax.ShapeDtypeStruct(shape, jnp.bfloat16) for shape in shapes],
        in_specs=[SMEM, SMEM, VMEM, VMEM, HBM],
        out_specs=[VMEM] * len(shapes),
        scratch_shapes=half_scratch(tokens, g_wide) + [pltpu.VMEM((extra, sum(cuts)), jnp.bfloat16)],
        compiler_params=limit(16),
    )(flags, lengths, act, f_in, grad)


def own_kernel(lengths_ref, act_ref, grad_ref, f_in, f_out, _, out, a_buf, a_sems, g_buf, g_sems):
    half = lax.axis_index("dp")
    sides = (
        (fetch_half(half, act_ref, a_buf, a_sems), a_buf, f_in),
        (fetch_half(half, grad_ref, g_buf, g_sems), g_buf, f_out),
    )
    rows, columns = out.shape[0], f_in.shape[1]
    select = selection(lengths_ref, lengths_ref.shape[0], rows, a_buf.shape[0])
    for side, (copies, buf, factor) in enumerate(sides):
        total = jnp.zeros((rows, columns), jnp.float32)
        for copy, start, piece in copies:
            copy.wait()

            def block(i, total, buf=buf, start=start, factor=factor):
                at = pl.multiple_of(start + i * WIDE, WIDE)
                packed = pick(select, buf[:, pl.ds(at, WIDE)])
                return total + jnp.dot(
                    packed, factor[pl.ds(at, WIDE), :], preferred_element_type=jnp.float32
                )

            total = lax.fori_loop(0, piece // WIDE, block, total)
        out[:, side * columns : (side + 1) * columns] = total


def own_part(rows, lengths, act, grad, f_in, f_out, after, work):
    tokens, columns = act.shape[0], f_in.shape[1]
    return pl.pallas_call(
        own_kernel,
        out_shape=jax.ShapeDtypeStruct((rows, 2 * columns), jnp.float32),
        in_specs=[SMEM, HBM, HBM, VMEM, VMEM, HBM],
        out_specs=VMEM,
        scratch_shapes=half_scratch(tokens, f_in.shape[0]) + half_scratch(tokens, f_out.shape[0]),
        compiler_params=limit(16),
        cost_estimate=pl.CostEstimate(flops=int(work * 1e9), bytes_accessed=0, transcendentals=0)
        if work
        else None,
    )(lengths, act, grad, f_in, f_out, after)


def encode(out, x):
    rows = x.shape[0]
    most = jnp.max(jnp.abs(x), axis=0, keepdims=True)
    power = jnp.ceil(jnp.log2(jnp.maximum(most, 2.0**-100)) + 0.01)
    whole = jnp.clip(jnp.round(x * jnp.exp2(15.0 - power)), -32767.0, 32767.0)
    out[:rows, :] = whole.astype(jnp.int32).astype(jnp.int16)
    out[rows:, :] = jnp.broadcast_to(power, (8, x.shape[1])).astype(jnp.int32).astype(jnp.int16)


def decode(ref, at, size, column, columns):
    rows, span = ref.shape[0] - 8, slice(column, column + columns)
    power = ref[rows : rows + 8, span].astype(jnp.int32).astype(jnp.float32)[:1]
    return ref[at : at + size, span].astype(jnp.int32).astype(jnp.float32) * jnp.exp2(power - 15.0)


def first_project_kernel(lent, x_ref, f_in, out):
    total = jnp.dot(x_ref[...], f_in[lent:, :], preferred_element_type=jnp.float32)
    if lent:
        out[...] = total
    else:
        encode(out, total)


def first_project(lent, x, f_in):
    rows, columns = x.shape[0], f_in.shape[1]
    return pl.pallas_call(
        functools.partial(first_project_kernel, lent),
        out_shape=jax.ShapeDtypeStruct((rows, columns), jnp.float32)
        if lent
        else jax.ShapeDtypeStruct((rows + 8, columns), jnp.int16),
        in_specs=[VMEM] * 2,
        out_specs=VMEM,
        compiler_params=limit(8),
    )(x, f_in)


def project_kernel(x_ref, f_out, out):
    out[...] = jnp.dot(x_ref[...], f_out[...], preferred_element_type=jnp.float32)


def project(x, f_out):
    rows, columns = x.shape[0], f_out.shape[1]
    return pl.pallas_call(
        project_kernel,
        out_shape=jax.ShapeDtypeStruct((rows, columns), jnp.float32),
        in_specs=[VMEM] * 2,
        out_specs=VMEM,
        compiler_params=limit(8),
    )(x, f_out)


def begin_kernel(x_ref, f_in, f_out, out):
    depth, columns = f_in.shape
    out[:, :columns] = jnp.dot(x_ref[:, :depth], f_in[...], preferred_element_type=jnp.float32)
    out[:, columns:] = jnp.dot(
        x_ref[:, depth:], f_out[: x_ref.shape[1] - depth, :], preferred_element_type=jnp.float32
    )


def begin(x, f_in, f_out):
    return pl.pallas_call(
        begin_kernel,
        out_shape=jax.ShapeDtypeStruct((x.shape[0], 2 * f_in.shape[1]), jnp.float32),
        in_specs=[VMEM] * 3,
        out_specs=VMEM,
        compiler_params=limit(8),
    )(x, f_in, f_out)


def finish_kernel(x_ref, made, f_out, out):
    depth, columns = f_out.shape
    outer = made[:, columns:] + jnp.dot(
        x_ref[...], f_out[depth - x_ref.shape[1] :, :], preferred_element_type=jnp.float32
    )
    encode(out, jnp.concatenate([made[:, :columns], outer], axis=1))


def finish(x, made, f_out):
    return pl.pallas_call(
        finish_kernel,
        out_shape=jax.ShapeDtypeStruct((x.shape[0] + 8, made.shape[1]), jnp.int16),
        in_specs=[VMEM] * 3,
        out_specs=VMEM,
        compiler_params=limit(8),
    )(x, made, f_out)


def extra_kernel(lent, base, flags_ref, made, act, f_in, f_out, *rest):
    pieces, (back, added, total, a_buf, f_buf, x_ref) = rest[:-6], rest[-6:]
    extra, (width, columns) = x_ref.shape[0], f_in.shape
    rows = base + extra
    row = 0
    for piece in pieces:
        x_ref[row : row + piece.shape[0], :] = piece[...]
        row += piece.shape[0]
    borrower = flags_ref[1] == 1

    @pl.when(borrower)
    def _():
        column = 0
        for at, size in blocks_of(base, extra):
            a_buf[at : at + size, :] = x_ref[:size, column : column + lent]
            column += lent
        for at, size in blocks_of(lent, extra):
            f_buf[at : at + size, :] = x_ref[:size, column : column + columns]
            column += columns
        total[:base, :] = made[...] + jnp.dot(
            a_buf[...], f_in[:lent, :], preferred_element_type=jnp.float32
        )
        total[base:, :] = jnp.zeros((2 * extra, columns), jnp.float32)
        added[...] = jnp.dot(act[:rows, :lent], f_buf[...], preferred_element_type=jnp.float32)

    @pl.when(jnp.logical_not(borrower))
    def _():
        total[:base, :] = made[...]
        total[base:rows, :] = jnp.dot(
            x_ref[:, : width - lent], f_in[lent:, :], preferred_element_type=jnp.float32
        )
        total[rows:, :] = jnp.dot(
            x_ref[:, width - lent :], f_out[...], preferred_element_type=jnp.float32
        )
        added[...] = jnp.zeros((rows, columns), jnp.float32)

    encode(back, total[...])


def extra_rows(lent, flags, made, pieces, act, f_in, f_out):
    base, extra, columns = made.shape[0], sum(x.shape[0] for x in pieces), f_in.shape[1]
    return pl.pallas_call(
        functools.partial(extra_kernel, lent, base),
        out_shape=[
            jax.ShapeDtypeStruct((base + 2 * extra + 8, columns), jnp.int16),
            jax.ShapeDtypeStruct((base + extra, columns), jnp.float32),
        ],
        in_specs=[SMEM] + [VMEM] * (4 + len(pieces)),
        out_specs=[VMEM, VMEM],
        scratch_shapes=[
            pltpu.VMEM((base + 2 * extra, columns), jnp.float32),
            pltpu.VMEM((base, lent), jnp.bfloat16),
            pltpu.VMEM((lent, columns), jnp.bfloat16),
            pltpu.VMEM((extra, pieces[0].shape[1]), jnp.bfloat16),
        ],
        compiler_params=limit(8),
    )(flags, made, act, f_in, f_out, *pieces)


def score_kernel(spans, lengths_ref, *rest):
    arrays, out_ref = rest[:-1], rest[-1]
    columns, sequences = QUERIES * RANK, lengths_ref.shape[0]
    sums = [jnp.zeros((1, columns), jnp.float32) for _ in range(sequences)]
    for first, size, sides in spans:
        total = [
            sum(
                decode(arrays[which], at, size, column, columns)
                if arrays[which].dtype == jnp.int16
                else arrays[which][at : at + size, column : column + columns]
                for which, at, column in parts
            )
            for parts in sides
        ]
        product = total[0] * total[1]
        row = first + lax.broadcasted_iota(jnp.int32, (size, columns), 0)
        before = jnp.int32(0)
        for s in range(sequences):
            after = before + lengths_ref[s]
            mine = (row >= before) & (row < after)
            sums[s] += jnp.sum(jnp.where(mine, product, 0.0), axis=0, keepdims=True)
            before = after
    total = jnp.concatenate(sums, axis=0)
    out_ref[...] = jnp.concatenate(
        [jnp.sum(total[:, q * RANK : (q + 1) * RANK], axis=1, keepdims=True) for q in range(QUERIES)],
        axis=1,
    )


def score(spans, lengths, arrays):
    return pl.pallas_call(
        functools.partial(score_kernel, spans),
        out_shape=jax.ShapeDtypeStruct((lengths.shape[0], QUERIES), jnp.float32),
        in_specs=[SMEM] + [VMEM] * len(arrays),
        out_specs=VMEM,
        compiler_params=limit(4),
    )(lengths, *arrays)


def lendable(base, extra, columns, a_wide, g_wide):
    best = 0
    for lent in range(128, a_wide, 128):
        used = len(blocks_of(base, extra)) * lent + len(blocks_of(lent, extra)) * columns
        if used <= a_wide - lent + g_wide:
            best = lent
    return best


def swap(x):
    return lax.ppermute(x, "dp", SWAP)


def swapped_scores(rows, base, lent, chunks, flags, lengths, packed, act, grad, f_in, f_out):
    columns, extra = f_in.shape[1], rows - base
    first = swap(packed[:base, lent:])
    width = f_in.shape[0] - lent + f_out.shape[0]
    cuts = [width] if lent else [f_in.shape[0] + LEAD, f_out.shape[0] - LEAD]
    sent = rest_rows(chunks, extra, cuts, lent, flags, lengths, packed, f_in, grad)
    groups = list(zip(sent, [sum(chunks[:i]) for i in range(len(chunks))] + [base] * len(cuts)))
    groups.sort(key=lambda group: -group[0].size)
    arrived = [swap(x) for x, _ in groups]
    if lent:
        made = first_project(lent, first, f_in)
        done = own = own_part(rows, lengths, act, grad, f_in, f_out, made, 1.7 if extra <= 3 * STEP else 2.9)
    else:
        own = own_part(rows, lengths, act, grad, f_in, f_out, lengths, 0)
        first, own = lax.optimization_barrier((first, own))
        done = made = first_project(lent, first, f_in)
    arrays, spans, in_parts = [own], [], [0]
    if not lent:
        in_parts.append(len(arrays))
        arrays.append(swap(made))
    for x, (_, at) in zip(arrived, groups):
        x, done = lax.optimization_barrier((x, done))
        here = len(arrays)
        if at < base:
            done = project(x, f_out)
            spans.append((at, x.shape[0], (here, 0, 0)))
        elif not lent and x.shape[1] == cuts[0]:
            done = begun = begin(x, f_in, f_out)
            continue
        elif not lent:
            done = finish(x, begun, f_out)
            spans.append((at, extra, (here, 0, columns)))
        else:
            done, added = extra_rows(lent, flags, made, [x], packed, f_in, f_out)
            in_parts += [here, here + 1]
            spans.append((at, extra, (here, rows, 0)))
        arrays.append(swap(done))
        if lent and at == base:
            arrays.append(added)
    spans = [
        (
            at,
            size,
            (
                ((0, at, 0), (back[0], 0, 0))
                if at == base and not lent
                else tuple((which, at, 0) for which in in_parts),
                ((0, at, columns), back),
            ),
        )
        for at, size, back in spans
    ]
    return score(spans, lengths, arrays)


def plan(rows, even, a_wide, g_wide, columns):
    if rows <= even + STEP:
        base = even - STEP
        large = (base + STEP) // 2 // STEP * STEP
        return rows, base, 0, [large, base - large]
    base = even - STEP
    large = (base + STEP) // 2 // STEP * STEP
    lent = lendable(base, rows - base, columns, a_wide, g_wide)
    return rows, base, lent, [large, base - STEP - large, STEP]


def layer_sum(x):
    size = lax.axis_size("layer")
    if size & (size - 1):
        return lax.psum(x, "layer")
    bits = [1 << i for i in range(size.bit_length() - 1)]
    steps = [bits[:1], bits[1:3], *([b] for b in bits[3:])]
    for step in steps:
        flips = [0]
        for bit in step:
            flips += [flip ^ bit for flip in flips]
        x = sum((lax.ppermute(x, "layer", [(i, i ^ flip) for i in range(size)]) for flip in flips[1:]), x)
    return x


def shards(activations, gradients, input_factor, output_factor, lengths):
    tokens = activations.shape[1]
    parts = lax.axis_size("dp")
    widths = (input_factor.shape[1], output_factor.shape[1])
    if parts == 2 and all(w % (2 * WIDE) == 0 for w in widths) and widths[1] > 2 * LEAD:
        act, grad, f_in, f_out = (x[0] for x in (activations, gradients, input_factor, output_factor))
        total = 5 * parts * tokens // 8
        even = (total // 2 + STEP - 1) // STEP * STEP
        sizes = [n for n in range(even, tokens, STEP) if n <= even + MOST * STEP] + [tokens]
        bounds = sizes[:-1]
        packed, flags = first_rows(total, bounds, lengths, act)
        plans = [plan(rows, even, *widths, f_in.shape[1]) for rows in sizes]
        per_sequence = lax.switch(
            flags[0],
            [functools.partial(swapped_scores, *p) for p in plans],
            *(flags, lengths, packed, act, grad, f_in, f_out),
        )
    else:
        per_sequence = gathered_scores(activations, gradients, input_factor, output_factor, lengths)
    blocks = lax.axis_size("layer")
    return layer_sum(per_sequence) / jnp.float32(math.sqrt(RANK * SLOT * blocks))


def solution(mesh):
    in_specs = (
        P("layer", "dp", None),
        P("layer", "dp", None),
        P("layer", "dp", None),
        P("layer", "dp", None),
        P("dp"),
    )
    out_specs = P("dp", None)
    return jax.shard_map(shards, mesh=mesh, in_specs=in_specs, out_specs=out_specs, check_vma=False)
```

```python
import functools
import math

import jax
import jax.numpy as jnp
from jax import lax
from jax.experimental import pallas as pl
from jax.experimental.pallas import tpu as pltpu
from jax.sharding import PartitionSpec as P

RANK = 32
QUERIES = 8
SLOT = 32
STEP = 8
WIDE = 512
MOST = 3
LEAD = 2048
SWAP = [(0, 1), (1, 0)]


def live_tokens(lengths, count):
    position = jnp.arange(count, dtype=jnp.int32)
    sequence = position // SLOT
    owners = sequence[:, None] == jnp.arange(lengths.shape[0], dtype=jnp.int32)[None, :]
    limit = jnp.sum(jnp.where(owners, lengths[None, :], 0), axis=1)
    return (position % SLOT < limit).astype(jnp.float32)


def rank_sum(first, second):
    return jnp.sum((first * second).reshape(first.shape[0], QUERIES, RANK), axis=2)


def gathered_scores(activations, gradients, input_factor, output_factor, lengths):
    tokens = activations.shape[1]
    projected_in = jnp.dot(
        activations[0],
        lax.all_gather(input_factor, "dp", axis=1, tiled=True)[0],
        preferred_element_type=jnp.float32,
    )
    projected_out = jnp.dot(
        gradients[0],
        lax.all_gather(output_factor, "dp", axis=1, tiled=True)[0],
        preferred_element_type=jnp.float32,
    )
    token_score = rank_sum(projected_out, projected_in)
    live = live_tokens(lengths, tokens)
    return jnp.sum(
        (token_score * live[:, None]).reshape(lengths.shape[0], SLOT, QUERIES), axis=1
    )


def selection(lengths_ref, sequences, rows, tokens):
    row = lax.broadcasted_iota(jnp.int32, (rows, tokens), 0)
    slot = lax.broadcasted_iota(jnp.int32, (rows, tokens), 1)
    picked = jnp.zeros((rows, tokens), jnp.bool_)
    before = jnp.int32(0)
    for s in range(sequences):
        length = lengths_ref[s]
        inside = slot - s * SLOT
        picked |= (inside >= 0) & (inside < length) & (row == before + inside)
        before += length
    return jnp.where(picked, 1.0, 0.0).astype(jnp.bfloat16)


VMEM = pl.BlockSpec(memory_space=pltpu.VMEM)
SMEM = pl.BlockSpec(memory_space=pltpu.SMEM)
HBM = pl.BlockSpec(memory_space=pl.ANY)


def limit(mib):
    return pltpu.CompilerParams(vmem_limit_bytes=mib * 1024 * 1024)


def fetch_half(half, ref, buf, sems, parts=2):
    width = buf.shape[1]
    piece = width // parts
    copies = []
    for p in range(parts):
        start = pl.multiple_of(half * width + p * piece, 128)
        copy = pltpu.make_async_copy(
            ref.at[:, pl.ds(start, piece)], buf.at[:, pl.ds(p * piece, piece)], sems.at[p]
        )
        copy.start()
        copies.append((copy, p * piece, piece))
    return copies


def half_scratch(tokens, width):
    return [pltpu.VMEM((tokens, width), jnp.bfloat16), pltpu.SemaphoreType.DMA((2,))]


def pick(select, block):
    return jnp.dot(select, block, preferred_element_type=jnp.float32).astype(jnp.bfloat16)


def first_kernel(total, bounds, lengths_ref, act_ref, out, flags_ref, buf, sems):
    copies = fetch_half(1 - lax.axis_index("dp"), act_ref, buf, sems, 1)
    sequences = lengths_ref.shape[0]
    live = jnp.int32(0)
    for s in range(sequences):
        live += lengths_ref[s]
    most = jnp.maximum(live, total - live)
    which = jnp.int32(0)
    for bound in bounds:
        which += (most > bound).astype(jnp.int32)
    flags_ref[0] = which
    flags_ref[1] = (live > total - live).astype(jnp.int32)
    select = selection(lengths_ref, sequences, out.shape[0], buf.shape[0])
    for copy, start, piece in copies:
        copy.wait()
        out[:, start : start + piece] = pick(select, buf[:, start : start + piece])


def first_rows(total, bounds, lengths, act):
    tokens, width = act.shape[0], act.shape[1] // 2
    return pl.pallas_call(
        functools.partial(first_kernel, total, bounds),
        out_shape=[
            jax.ShapeDtypeStruct((tokens, width), jnp.bfloat16),
            jax.ShapeDtypeStruct((2,), jnp.int32),
        ],
        in_specs=[SMEM, HBM],
        out_specs=[VMEM, SMEM],
        scratch_shapes=half_scratch(tokens, width),
        compiler_params=limit(8),
    )(lengths, act)


def blocks_of(rows, size):
    return [(at, min(size, rows - at)) for at in range(0, rows, size)]


def rest_kernel(chunks, extra, cuts, lent, flags_ref, lengths_ref, act, f_in, grad_ref, *rest):
    outs, (buf, sems, wide) = rest[:-3], rest[-3:]
    copies = fetch_half(1 - lax.axis_index("dp"), grad_ref, buf, sems)
    base, width = sum(chunks), act.shape[1]
    select = selection(lengths_ref, lengths_ref.shape[0], base + extra, buf.shape[0])
    lender = (flags_ref[1] == 0) & (lent > 0)
    if lent:

        @pl.when(lender)
        def _():
            column = 0
            for at, size in blocks_of(base, extra):
                wide[:size, column : column + lent] = act[at : at + size, :lent]
                column += lent
            for at, size in blocks_of(lent, extra):
                wide[:size, column : column + f_in.shape[1]] = f_in[at : at + size, :]
                column += f_in.shape[1]

    if extra:

        @pl.when(jnp.logical_not(lender))
        def _():
            wide[:, : width - lent] = act[base : base + extra, lent:]

    for copy, start, piece in copies:
        copy.wait()

        def block(i, _, start=start):
            at = pl.multiple_of(start + i * WIDE, WIDE)
            packed = pick(select, buf[:, pl.ds(at, WIDE)])
            row = 0
            for out, size in zip(outs, chunks):
                out[:, pl.ds(at, WIDE)] = packed[row : row + size]
                row += size
            if extra:

                @pl.when(jnp.logical_not(lender))
                def _():
                    wide[:, pl.ds(width - lent + at, WIDE)] = packed[row:]

            return 0

        lax.fori_loop(0, piece // WIDE, block, 0)
    column = 0
    for out, size in zip(outs[len(chunks) :], cuts):
        out[...] = wide[:, column : column + size]
        column += size


def rest_rows(chunks, extra, cuts, lent, flags, lengths, act, f_in, grad):
    tokens, a_wide, g_wide = grad.shape[0], act.shape[1], grad.shape[1] // 2
    shapes = [(n, g_wide) for n in chunks] + [(extra, n) for n in cuts]
    return pl.pallas_call(
        functools.partial(rest_kernel, chunks, extra, cuts, lent),
        out_shape=[jax.ShapeDtypeStruct(shape, jnp.bfloat16) for shape in shapes],
        in_specs=[SMEM, SMEM, VMEM, VMEM, HBM],
        out_specs=[VMEM] * len(shapes),
        scratch_shapes=half_scratch(tokens, g_wide) + [pltpu.VMEM((extra, sum(cuts)), jnp.bfloat16)],
        compiler_params=limit(16),
    )(flags, lengths, act, f_in, grad)


def own_kernel(lengths_ref, act_ref, grad_ref, f_in, f_out, _, out, a_buf, a_sems, g_buf, g_sems):
    half = lax.axis_index("dp")
    sides = (
        (fetch_half(half, act_ref, a_buf, a_sems), a_buf, f_in),
        (fetch_half(half, grad_ref, g_buf, g_sems), g_buf, f_out),
    )
    rows, columns = out.shape[0], f_in.shape[1]
    select = selection(lengths_ref, lengths_ref.shape[0], rows, a_buf.shape[0])
    for side, (copies, buf, factor) in enumerate(sides):
        total = jnp.zeros((rows, columns), jnp.float32)
        for copy, start, piece in copies:
            copy.wait()

            def block(i, total, buf=buf, start=start, factor=factor):
                at = pl.multiple_of(start + i * WIDE, WIDE)
                packed = pick(select, buf[:, pl.ds(at, WIDE)])
                return total + jnp.dot(
                    packed, factor[pl.ds(at, WIDE), :], preferred_element_type=jnp.float32
                )

            total = lax.fori_loop(0, piece // WIDE, block, total)
        out[:, side * columns : (side + 1) * columns] = total


def own_part(rows, lengths, act, grad, f_in, f_out, after, work):
    tokens, columns = act.shape[0], f_in.shape[1]
    return pl.pallas_call(
        own_kernel,
        out_shape=jax.ShapeDtypeStruct((rows, 2 * columns), jnp.float32),
        in_specs=[SMEM, HBM, HBM, VMEM, VMEM, HBM],
        out_specs=VMEM,
        scratch_shapes=half_scratch(tokens, f_in.shape[0]) + half_scratch(tokens, f_out.shape[0]),
        compiler_params=limit(16),
        cost_estimate=pl.CostEstimate(flops=int(work * 1e9), bytes_accessed=0, transcendentals=0)
        if work
        else None,
    )(lengths, act, grad, f_in, f_out, after)


def encode(out, x):
    rows = x.shape[0]
    most = jnp.max(jnp.abs(x), axis=0, keepdims=True)
    power = jnp.ceil(jnp.log2(jnp.maximum(most, 2.0**-100)) + 0.01)
    whole = jnp.clip(jnp.round(x * jnp.exp2(15.0 - power)), -32767.0, 32767.0)
    out[:rows, :] = whole.astype(jnp.int32).astype(jnp.int16)
    out[rows:, :] = jnp.broadcast_to(power, (8, x.shape[1])).astype(jnp.int32).astype(jnp.int16)


def decode(ref, at, size, column, columns):
    rows, span = ref.shape[0] - 8, slice(column, column + columns)
    power = ref[rows : rows + 8, span].astype(jnp.int32).astype(jnp.float32)[:1]
    return ref[at : at + size, span].astype(jnp.int32).astype(jnp.float32) * jnp.exp2(power - 15.0)


def first_project_kernel(lent, x_ref, f_in, out):
    total = jnp.dot(x_ref[...], f_in[lent:, :], preferred_element_type=jnp.float32)
    if lent:
        out[...] = total
    else:
        encode(out, total)


def first_project(lent, x, f_in):
    rows, columns = x.shape[0], f_in.shape[1]
    return pl.pallas_call(
        functools.partial(first_project_kernel, lent),
        out_shape=jax.ShapeDtypeStruct((rows, columns), jnp.float32)
        if lent
        else jax.ShapeDtypeStruct((rows + 8, columns), jnp.int16),
        in_specs=[VMEM] * 2,
        out_specs=VMEM,
        compiler_params=limit(8),
    )(x, f_in)


def project_kernel(x_ref, f_out, out):
    out[...] = jnp.dot(x_ref[...], f_out[...], preferred_element_type=jnp.float32)


def project(x, f_out):
    rows, columns = x.shape[0], f_out.shape[1]
    return pl.pallas_call(
        project_kernel,
        out_shape=jax.ShapeDtypeStruct((rows, columns), jnp.float32),
        in_specs=[VMEM] * 2,
        out_specs=VMEM,
        compiler_params=limit(8),
    )(x, f_out)


def begin_kernel(x_ref, f_in, f_out, out):
    depth, columns = f_in.shape
    out[:, :columns] = jnp.dot(x_ref[:, :depth], f_in[...], preferred_element_type=jnp.float32)
    out[:, columns:] = jnp.dot(
        x_ref[:, depth:], f_out[: x_ref.shape[1] - depth, :], preferred_element_type=jnp.float32
    )


def begin(x, f_in, f_out):
    return pl.pallas_call(
        begin_kernel,
        out_shape=jax.ShapeDtypeStruct((x.shape[0], 2 * f_in.shape[1]), jnp.float32),
        in_specs=[VMEM] * 3,
        out_specs=VMEM,
        compiler_params=limit(8),
    )(x, f_in, f_out)


def part_kernel(x_ref, f_out, out):
    out[...] = jnp.dot(x_ref[...], f_out[: x_ref.shape[1], :], preferred_element_type=jnp.float32)


def part(x, f_out):
    return pl.pallas_call(
        part_kernel,
        out_shape=jax.ShapeDtypeStruct((x.shape[0], f_out.shape[1]), jnp.float32),
        in_specs=[VMEM] * 2,
        out_specs=VMEM,
        compiler_params=limit(8),
    )(x, f_out)


def whole_kernel(x_ref, made, f_out, out):
    rest = f_out.shape[0] - x_ref.shape[1]
    encode(out, made[...] + jnp.dot(x_ref[...], f_out[rest:, :], preferred_element_type=jnp.float32))


def whole(x, made, f_out):
    return pl.pallas_call(
        whole_kernel,
        out_shape=jax.ShapeDtypeStruct((x.shape[0] + 8, f_out.shape[1]), jnp.int16),
        in_specs=[VMEM] * 3,
        out_specs=VMEM,
        compiler_params=limit(8),
    )(x, made, f_out)


def finish_kernel(x_ref, made, f_out, out):
    depth, columns = f_out.shape
    outer = made[:, columns:] + jnp.dot(
        x_ref[...], f_out[depth - x_ref.shape[1] :, :], preferred_element_type=jnp.float32
    )
    encode(out, jnp.concatenate([made[:, :columns], outer], axis=1))


def finish(x, made, f_out):
    return pl.pallas_call(
        finish_kernel,
        out_shape=jax.ShapeDtypeStruct((x.shape[0] + 8, made.shape[1]), jnp.int16),
        in_specs=[VMEM] * 3,
        out_specs=VMEM,
        compiler_params=limit(8),
    )(x, made, f_out)


def extra_kernel(lent, base, flags_ref, made, act, f_in, f_out, *rest):
    pieces, (back, added, total, a_buf, f_buf, x_ref) = rest[:-6], rest[-6:]
    extra, (width, columns) = x_ref.shape[0], f_in.shape
    rows = base + extra
    row = 0
    for piece in pieces:
        x_ref[row : row + piece.shape[0], :] = piece[...]
        row += piece.shape[0]
    borrower = flags_ref[1] == 1

    @pl.when(borrower)
    def _():
        column = 0
        for at, size in blocks_of(base, extra):
            a_buf[at : at + size, :] = x_ref[:size, column : column + lent]
            column += lent
        for at, size in blocks_of(lent, extra):
            f_buf[at : at + size, :] = x_ref[:size, column : column + columns]
            column += columns
        total[:base, :] = made[...] + jnp.dot(
            a_buf[...], f_in[:lent, :], preferred_element_type=jnp.float32
        )
        total[base:, :] = jnp.zeros((2 * extra, columns), jnp.float32)
        added[...] = jnp.dot(act[:rows, :lent], f_buf[...], preferred_element_type=jnp.float32)

    @pl.when(jnp.logical_not(borrower))
    def _():
        total[:base, :] = made[...]
        total[base:rows, :] = jnp.dot(
            x_ref[:, : width - lent], f_in[lent:, :], preferred_element_type=jnp.float32
        )
        total[rows:, :] = jnp.dot(
            x_ref[:, width - lent :], f_out[...], preferred_element_type=jnp.float32
        )
        added[...] = jnp.zeros((rows, columns), jnp.float32)

    encode(back, total[...])


def extra_rows(lent, flags, made, pieces, act, f_in, f_out):
    base, extra, columns = made.shape[0], sum(x.shape[0] for x in pieces), f_in.shape[1]
    return pl.pallas_call(
        functools.partial(extra_kernel, lent, base),
        out_shape=[
            jax.ShapeDtypeStruct((base + 2 * extra + 8, columns), jnp.int16),
            jax.ShapeDtypeStruct((base + extra, columns), jnp.float32),
        ],
        in_specs=[SMEM] + [VMEM] * (4 + len(pieces)),
        out_specs=[VMEM, VMEM],
        scratch_shapes=[
            pltpu.VMEM((base + 2 * extra, columns), jnp.float32),
            pltpu.VMEM((base, lent), jnp.bfloat16),
            pltpu.VMEM((lent, columns), jnp.bfloat16),
            pltpu.VMEM((extra, pieces[0].shape[1]), jnp.bfloat16),
        ],
        compiler_params=limit(8),
    )(flags, made, act, f_in, f_out, *pieces)


def score_kernel(spans, lengths_ref, *rest):
    arrays, out_ref = rest[:-1], rest[-1]
    columns, sequences = QUERIES * RANK, lengths_ref.shape[0]
    sums = [jnp.zeros((1, columns), jnp.float32) for _ in range(sequences)]
    for first, size, sides in spans:
        total = [
            sum(
                decode(arrays[which], at, size, column, columns)
                if arrays[which].dtype == jnp.int16
                else arrays[which][at : at + size, column : column + columns]
                for which, at, column in parts
            )
            for parts in sides
        ]
        product = total[0] * total[1]
        row = first + lax.broadcasted_iota(jnp.int32, (size, columns), 0)
        before = jnp.int32(0)
        for s in range(sequences):
            after = before + lengths_ref[s]
            mine = (row >= before) & (row < after)
            sums[s] += jnp.sum(jnp.where(mine, product, 0.0), axis=0, keepdims=True)
            before = after
    total = jnp.concatenate(sums, axis=0)
    out_ref[...] = jnp.concatenate(
        [jnp.sum(total[:, q * RANK : (q + 1) * RANK], axis=1, keepdims=True) for q in range(QUERIES)],
        axis=1,
    )


def score(spans, lengths, arrays):
    return pl.pallas_call(
        functools.partial(score_kernel, spans),
        out_shape=jax.ShapeDtypeStruct((lengths.shape[0], QUERIES), jnp.float32),
        in_specs=[SMEM] + [VMEM] * len(arrays),
        out_specs=VMEM,
        compiler_params=limit(4),
    )(lengths, *arrays)


def lendable(base, extra, columns, a_wide, g_wide):
    best = 0
    for lent in range(128, a_wide, 128):
        used = len(blocks_of(base, extra)) * lent + len(blocks_of(lent, extra)) * columns
        if used <= a_wide - lent + g_wide:
            best = lent
    return best


def swap(x):
    return lax.ppermute(x, "dp", SWAP)


def swapped_scores(rows, base, lent, chunks, flags, lengths, packed, act, grad, f_in, f_out):
    columns, extra = f_in.shape[1], rows - base
    first = swap(packed[:base, lent:])
    width = f_in.shape[0] - lent + f_out.shape[0]
    cuts = [width] if lent else [f_in.shape[0] + LEAD, f_out.shape[0] - LEAD]
    sent = rest_rows(chunks, extra, cuts, lent, flags, lengths, packed, f_in, grad)
    groups = list(zip(sent, [sum(chunks[:i]) for i in range(len(chunks))] + [base] * len(cuts)))
    if lent:
        x, at = groups.pop(1)
        groups += [(x[:, :-LEAD], at), (x[:, -LEAD:], at)]
    groups.sort(key=lambda group: -group[0].size)
    arrived = [swap(x) for x, _ in groups]
    if lent:
        made = first_project(lent, first, f_in)
        done = own = own_part(rows, lengths, act, grad, f_in, f_out, made, 1.7 if extra <= 3 * STEP else 2.9)
    else:
        own = own_part(rows, lengths, act, grad, f_in, f_out, lengths, 0)
        first, own = lax.optimization_barrier((first, own))
        done = made = first_project(lent, first, f_in)
    arrays, spans, in_parts = [own], [], [0]
    if not lent:
        in_parts.append(len(arrays))
        arrays.append(swap(made))
    for x, (_, at) in zip(arrived, groups):
        x, done = lax.optimization_barrier((x, done))
        here = len(arrays)
        if at < base and x.shape[1] == f_out.shape[0] - LEAD:
            done = begun = part(x, f_out)
            continue
        if at < base and x.shape[1] == LEAD:
            done = whole(x, begun, f_out)
            spans.append((at, x.shape[0], (here, 0, 0)))
        elif at < base:
            done = project(x, f_out)
            spans.append((at, x.shape[0], (here, 0, 0)))
        elif not lent and x.shape[1] == cuts[0]:
            done = begun = begin(x, f_in, f_out)
            continue
        elif not lent:
            done = finish(x, begun, f_out)
            spans.append((at, extra, (here, 0, columns)))
        else:
            done, added = extra_rows(lent, flags, made, [x], packed, f_in, f_out)
            in_parts += [here, here + 1]
            spans.append((at, extra, (here, rows, 0)))
        arrays.append(swap(done))
        if lent and at == base:
            arrays.append(added)
    spans = [
        (
            at,
            size,
            (
                ((0, at, 0), (back[0], 0, 0))
                if at == base and not lent
                else tuple((which, at, 0) for which in in_parts),
                ((0, at, columns), back),
            ),
        )
        for at, size, back in spans
    ]
    return score(spans, lengths, arrays)


def plan(rows, even, a_wide, g_wide, columns):
    if rows <= even + STEP:
        base = even - STEP
        large = (base + STEP) // 2 // STEP * STEP
        return rows, base, 0, [large, base - large]
    base = even - STEP
    large = (base + STEP) // 2 // STEP * STEP
    lent = lendable(base, rows - base, columns, a_wide, g_wide)
    return rows, base, lent, [large, base - large]


def layer_sum(x):
    size = lax.axis_size("layer")
    if size & (size - 1):
        return lax.psum(x, "layer")
    bits = [1 << i for i in range(size.bit_length() - 1)]
    steps = [bits[:1], bits[1:3], *([b] for b in bits[3:])]
    for step in steps:
        flips = [0]
        for bit in step:
            flips += [flip ^ bit for flip in flips]
        x = sum((lax.ppermute(x, "layer", [(i, i ^ flip) for i in range(size)]) for flip in flips[1:]), x)
    return x


def shards(activations, gradients, input_factor, output_factor, lengths):
    tokens = activations.shape[1]
    parts = lax.axis_size("dp")
    widths = (input_factor.shape[1], output_factor.shape[1])
    if parts == 2 and all(w % (2 * WIDE) == 0 for w in widths) and widths[1] > 2 * LEAD:
        act, grad, f_in, f_out = (x[0] for x in (activations, gradients, input_factor, output_factor))
        total = 5 * parts * tokens // 8
        even = (total // 2 + STEP - 1) // STEP * STEP
        sizes = [n for n in range(even, tokens, STEP) if n <= even + MOST * STEP] + [tokens]
        bounds = sizes[:-1]
        packed, flags = first_rows(total, bounds, lengths, act)
        plans = [plan(rows, even, *widths, f_in.shape[1]) for rows in sizes]
        per_sequence = lax.switch(
            flags[0],
            [functools.partial(swapped_scores, *p) for p in plans],
            *(flags, lengths, packed, act, grad, f_in, f_out),
        )
    else:
        per_sequence = gathered_scores(activations, gradients, input_factor, output_factor, lengths)
    blocks = lax.axis_size("layer")
    return layer_sum(per_sequence) / jnp.float32(math.sqrt(RANK * SLOT * blocks))


def solution(mesh):
    in_specs = (
        P("layer", "dp", None),
        P("layer", "dp", None),
        P("layer", "dp", None),
        P("layer", "dp", None),
        P("dp"),
    )
    out_specs = P("dp", None)
    return jax.shard_map(shards, mesh=mesh, in_specs=in_specs, out_specs=out_specs, check_vma=False)
```

```python
import functools
import math

import jax
import jax.numpy as jnp
from jax import lax
from jax.experimental import pallas as pl
from jax.experimental.pallas import tpu as pltpu
from jax.sharding import PartitionSpec as P

RANK = 32
QUERIES = 8
SLOT = 32
STEP = 8
WIDE = 512
MOST = 3
LEAD = 2048
SWAP = [(0, 1), (1, 0)]


def live_tokens(lengths, count):
    position = jnp.arange(count, dtype=jnp.int32)
    sequence = position // SLOT
    owners = sequence[:, None] == jnp.arange(lengths.shape[0], dtype=jnp.int32)[None, :]
    limit = jnp.sum(jnp.where(owners, lengths[None, :], 0), axis=1)
    return (position % SLOT < limit).astype(jnp.float32)


def rank_sum(first, second):
    return jnp.sum((first * second).reshape(first.shape[0], QUERIES, RANK), axis=2)


def gathered_scores(activations, gradients, input_factor, output_factor, lengths):
    tokens = activations.shape[1]
    projected_in = jnp.dot(
        activations[0],
        lax.all_gather(input_factor, "dp", axis=1, tiled=True)[0],
        preferred_element_type=jnp.float32,
    )
    projected_out = jnp.dot(
        gradients[0],
        lax.all_gather(output_factor, "dp", axis=1, tiled=True)[0],
        preferred_element_type=jnp.float32,
    )
    token_score = rank_sum(projected_out, projected_in)
    live = live_tokens(lengths, tokens)
    return jnp.sum(
        (token_score * live[:, None]).reshape(lengths.shape[0], SLOT, QUERIES), axis=1
    )


def selection(lengths_ref, sequences, rows, tokens):
    row = lax.broadcasted_iota(jnp.int32, (rows, tokens), 0)
    slot = lax.broadcasted_iota(jnp.int32, (rows, tokens), 1)
    picked = jnp.zeros((rows, tokens), jnp.bool_)
    before = jnp.int32(0)
    for s in range(sequences):
        length = lengths_ref[s]
        inside = slot - s * SLOT
        picked |= (inside >= 0) & (inside < length) & (row == before + inside)
        before += length
    return jnp.where(picked, 1.0, 0.0).astype(jnp.bfloat16)


VMEM = pl.BlockSpec(memory_space=pltpu.VMEM)
SMEM = pl.BlockSpec(memory_space=pltpu.SMEM)
HBM = pl.BlockSpec(memory_space=pl.ANY)


def limit(mib):
    return pltpu.CompilerParams(vmem_limit_bytes=mib * 1024 * 1024)


def fetch_half(half, ref, buf, sems, parts=2):
    width = buf.shape[1]
    piece = width // parts
    copies = []
    for p in range(parts):
        start = pl.multiple_of(half * width + p * piece, 128)
        copy = pltpu.make_async_copy(
            ref.at[:, pl.ds(start, piece)], buf.at[:, pl.ds(p * piece, piece)], sems.at[p]
        )
        copy.start()
        copies.append((copy, p * piece, piece))
    return copies


def half_scratch(tokens, width):
    return [pltpu.VMEM((tokens, width), jnp.bfloat16), pltpu.SemaphoreType.DMA((2,))]


def pick(select, block):
    return jnp.dot(select, block, preferred_element_type=jnp.float32).astype(jnp.bfloat16)


def first_kernel(total, bounds, lengths_ref, act_ref, out, flags_ref, buf, sems):
    copies = fetch_half(1 - lax.axis_index("dp"), act_ref, buf, sems, 1)
    sequences = lengths_ref.shape[0]
    live = jnp.int32(0)
    for s in range(sequences):
        live += lengths_ref[s]
    most = jnp.maximum(live, total - live)
    which = jnp.int32(0)
    for bound in bounds:
        which += (most > bound).astype(jnp.int32)
    flags_ref[0] = which
    flags_ref[1] = (live > total - live).astype(jnp.int32)
    select = selection(lengths_ref, sequences, out.shape[0], buf.shape[0])
    for copy, start, piece in copies:
        copy.wait()
        out[:, start : start + piece] = pick(select, buf[:, start : start + piece])


def first_rows(total, bounds, lengths, act):
    tokens, width = act.shape[0], act.shape[1] // 2
    return pl.pallas_call(
        functools.partial(first_kernel, total, bounds),
        out_shape=[
            jax.ShapeDtypeStruct((tokens, width), jnp.bfloat16),
            jax.ShapeDtypeStruct((2,), jnp.int32),
        ],
        in_specs=[SMEM, HBM],
        out_specs=[VMEM, SMEM],
        scratch_shapes=half_scratch(tokens, width),
        compiler_params=limit(8),
    )(lengths, act)


def blocks_of(rows, size):
    return [(at, min(size, rows - at)) for at in range(0, rows, size)]


def rest_kernel(chunks, extra, cuts, lent, flags_ref, lengths_ref, act, f_in, grad_ref, *rest):
    outs, (buf, sems, wide) = rest[:-3], rest[-3:]
    copies = fetch_half(1 - lax.axis_index("dp"), grad_ref, buf, sems)
    base, width = sum(chunks), act.shape[1]
    select = selection(lengths_ref, lengths_ref.shape[0], base + extra, buf.shape[0])
    lender = (flags_ref[1] == 0) & (lent > 0)
    if lent:

        @pl.when(lender)
        def _():
            column = 0
            for at, size in blocks_of(base, extra):
                wide[:size, column : column + lent] = act[at : at + size, :lent]
                column += lent
            for at, size in blocks_of(lent, extra):
                wide[:size, column : column + f_in.shape[1]] = f_in[at : at + size, :]
                column += f_in.shape[1]

    if extra:

        @pl.when(jnp.logical_not(lender))
        def _():
            wide[:, : width - lent] = act[base : base + extra, lent:]

    for copy, start, piece in copies:
        copy.wait()

        def block(i, _, start=start):
            at = pl.multiple_of(start + i * WIDE, WIDE)
            packed = pick(select, buf[:, pl.ds(at, WIDE)])
            row = 0
            for out, size in zip(outs, chunks):
                out[:, pl.ds(at, WIDE)] = packed[row : row + size]
                row += size
            if extra:

                @pl.when(jnp.logical_not(lender))
                def _():
                    wide[:, pl.ds(width - lent + at, WIDE)] = packed[row:]

            return 0

        lax.fori_loop(0, piece // WIDE, block, 0)
    column = 0
    for out, size in zip(outs[len(chunks) :], cuts):
        out[...] = wide[:, column : column + size]
        column += size


def rest_rows(chunks, extra, cuts, lent, flags, lengths, act, f_in, grad):
    tokens, a_wide, g_wide = grad.shape[0], act.shape[1], grad.shape[1] // 2
    shapes = [(n, g_wide) for n in chunks] + [(extra, n) for n in cuts]
    return pl.pallas_call(
        functools.partial(rest_kernel, chunks, extra, cuts, lent),
        out_shape=[jax.ShapeDtypeStruct(shape, jnp.bfloat16) for shape in shapes],
        in_specs=[SMEM, SMEM, VMEM, VMEM, HBM],
        out_specs=[VMEM] * len(shapes),
        scratch_shapes=half_scratch(tokens, g_wide) + [pltpu.VMEM((extra, sum(cuts)), jnp.bfloat16)],
        compiler_params=limit(16),
    )(flags, lengths, act, f_in, grad)


def own_kernel(lengths_ref, act_ref, grad_ref, f_in, f_out, _, out, a_buf, a_sems, g_buf, g_sems):
    half = lax.axis_index("dp")
    sides = (
        (fetch_half(half, act_ref, a_buf, a_sems), a_buf, f_in),
        (fetch_half(half, grad_ref, g_buf, g_sems), g_buf, f_out),
    )
    rows, columns = out.shape[0], f_in.shape[1]
    select = selection(lengths_ref, lengths_ref.shape[0], rows, a_buf.shape[0])
    for side, (copies, buf, factor) in enumerate(sides):
        total = jnp.zeros((rows, columns), jnp.float32)
        for copy, start, piece in copies:
            copy.wait()

            def block(i, total, buf=buf, start=start, factor=factor):
                at = pl.multiple_of(start + i * WIDE, WIDE)
                packed = pick(select, buf[:, pl.ds(at, WIDE)])
                return total + jnp.dot(
                    packed, factor[pl.ds(at, WIDE), :], preferred_element_type=jnp.float32
                )

            total = lax.fori_loop(0, piece // WIDE, block, total)
        out[:, side * columns : (side + 1) * columns] = total


def own_part(rows, lengths, act, grad, f_in, f_out, after, work):
    tokens, columns = act.shape[0], f_in.shape[1]
    return pl.pallas_call(
        own_kernel,
        out_shape=jax.ShapeDtypeStruct((rows, 2 * columns), jnp.float32),
        in_specs=[SMEM, HBM, HBM, VMEM, VMEM, HBM],
        out_specs=VMEM,
        scratch_shapes=half_scratch(tokens, f_in.shape[0]) + half_scratch(tokens, f_out.shape[0]),
        compiler_params=limit(16),
        cost_estimate=pl.CostEstimate(flops=int(work * 1e9), bytes_accessed=0, transcendentals=0)
        if work
        else None,
    )(lengths, act, grad, f_in, f_out, after)


def encode(out, x):
    rows = x.shape[0]
    most = jnp.max(jnp.abs(x), axis=0, keepdims=True)
    power = jnp.ceil(jnp.log2(jnp.maximum(most, 2.0**-100)) + 0.01)
    whole = jnp.clip(jnp.round(x * jnp.exp2(15.0 - power)), -32767.0, 32767.0)
    out[:rows, :] = whole.astype(jnp.int32).astype(jnp.int16)
    out[rows:, :] = jnp.broadcast_to(power, (8, x.shape[1])).astype(jnp.int32).astype(jnp.int16)


def decode(ref, at, size, column, columns):
    rows, span = ref.shape[0] - 8, slice(column, column + columns)
    power = ref[rows : rows + 8, span].astype(jnp.int32).astype(jnp.float32)[:1]
    return ref[at : at + size, span].astype(jnp.int32).astype(jnp.float32) * jnp.exp2(power - 15.0)


def first_project_kernel(lent, x_ref, f_in, out):
    total = jnp.dot(x_ref[...], f_in[lent:, :], preferred_element_type=jnp.float32)
    if lent:
        out[...] = total
    else:
        encode(out, total)


def first_project(lent, x, f_in):
    rows, columns = x.shape[0], f_in.shape[1]
    return pl.pallas_call(
        functools.partial(first_project_kernel, lent),
        out_shape=jax.ShapeDtypeStruct((rows, columns), jnp.float32)
        if lent
        else jax.ShapeDtypeStruct((rows + 8, columns), jnp.int16),
        in_specs=[VMEM] * 2,
        out_specs=VMEM,
        compiler_params=limit(8),
    )(x, f_in)


def project_kernel(x_ref, f_out, out):
    out[...] = jnp.dot(x_ref[...], f_out[...], preferred_element_type=jnp.float32)


def project(x, f_out):
    rows, columns = x.shape[0], f_out.shape[1]
    return pl.pallas_call(
        project_kernel,
        out_shape=jax.ShapeDtypeStruct((rows, columns), jnp.float32),
        in_specs=[VMEM] * 2,
        out_specs=VMEM,
        compiler_params=limit(8),
    )(x, f_out)


def begin_kernel(x_ref, f_in, f_out, out):
    depth, columns = f_in.shape
    out[:, :columns] = jnp.dot(x_ref[:, :depth], f_in[...], preferred_element_type=jnp.float32)
    out[:, columns:] = jnp.dot(
        x_ref[:, depth:], f_out[: x_ref.shape[1] - depth, :], preferred_element_type=jnp.float32
    )


def begin(x, f_in, f_out):
    return pl.pallas_call(
        begin_kernel,
        out_shape=jax.ShapeDtypeStruct((x.shape[0], 2 * f_in.shape[1]), jnp.float32),
        in_specs=[VMEM] * 3,
        out_specs=VMEM,
        compiler_params=limit(8),
    )(x, f_in, f_out)


def part_kernel(x_ref, f_out, out):
    out[...] = jnp.dot(x_ref[...], f_out[: x_ref.shape[1], :], preferred_element_type=jnp.float32)


def part(x, f_out):
    return pl.pallas_call(
        part_kernel,
        out_shape=jax.ShapeDtypeStruct((x.shape[0], f_out.shape[1]), jnp.float32),
        in_specs=[VMEM] * 2,
        out_specs=VMEM,
        compiler_params=limit(8),
    )(x, f_out)


def whole_kernel(x_ref, made, f_out, out):
    rest = f_out.shape[0] - x_ref.shape[1]
    encode(out, made[...] + jnp.dot(x_ref[...], f_out[rest:, :], preferred_element_type=jnp.float32))


def whole(x, made, f_out):
    return pl.pallas_call(
        whole_kernel,
        out_shape=jax.ShapeDtypeStruct((x.shape[0] + 8, f_out.shape[1]), jnp.int16),
        in_specs=[VMEM] * 3,
        out_specs=VMEM,
        compiler_params=limit(8),
    )(x, made, f_out)


def finish_kernel(x_ref, made, f_out, out):
    depth, columns = f_out.shape
    outer = made[:, columns:] + jnp.dot(
        x_ref[...], f_out[depth - x_ref.shape[1] :, :], preferred_element_type=jnp.float32
    )
    encode(out, jnp.concatenate([made[:, :columns], outer], axis=1))


def finish(x, made, f_out):
    return pl.pallas_call(
        finish_kernel,
        out_shape=jax.ShapeDtypeStruct((x.shape[0] + 8, made.shape[1]), jnp.int16),
        in_specs=[VMEM] * 3,
        out_specs=VMEM,
        compiler_params=limit(8),
    )(x, made, f_out)


def extra_kernel(lent, base, flags_ref, made, act, f_in, f_out, *rest):
    pieces, (back, added, total, a_buf, f_buf, x_ref) = rest[:-6], rest[-6:]
    extra, (width, columns) = x_ref.shape[0], f_in.shape
    rows = base + extra
    row = 0
    for piece in pieces:
        x_ref[row : row + piece.shape[0], :] = piece[...]
        row += piece.shape[0]
    borrower = flags_ref[1] == 1

    @pl.when(borrower)
    def _():
        column = 0
        for at, size in blocks_of(base, extra):
            a_buf[at : at + size, :] = x_ref[:size, column : column + lent]
            column += lent
        for at, size in blocks_of(lent, extra):
            f_buf[at : at + size, :] = x_ref[:size, column : column + columns]
            column += columns
        total[:base, :] = made[...] + jnp.dot(
            a_buf[...], f_in[:lent, :], preferred_element_type=jnp.float32
        )
        total[base:, :] = jnp.zeros((2 * extra, columns), jnp.float32)
        added[...] = jnp.dot(act[:rows, :lent], f_buf[...], preferred_element_type=jnp.float32)

    @pl.when(jnp.logical_not(borrower))
    def _():
        total[:base, :] = made[...]
        total[base:rows, :] = jnp.dot(
            x_ref[:, : width - lent], f_in[lent:, :], preferred_element_type=jnp.float32
        )
        total[rows:, :] = jnp.dot(
            x_ref[:, width - lent :], f_out[...], preferred_element_type=jnp.float32
        )
        added[...] = jnp.zeros((rows, columns), jnp.float32)

    encode(back, total[...])


def extra_rows(lent, flags, made, pieces, act, f_in, f_out):
    base, extra, columns = made.shape[0], sum(x.shape[0] for x in pieces), f_in.shape[1]
    return pl.pallas_call(
        functools.partial(extra_kernel, lent, base),
        out_shape=[
            jax.ShapeDtypeStruct((base + 2 * extra + 8, columns), jnp.int16),
            jax.ShapeDtypeStruct((base + extra, columns), jnp.float32),
        ],
        in_specs=[SMEM] + [VMEM] * (4 + len(pieces)),
        out_specs=[VMEM, VMEM],
        scratch_shapes=[
            pltpu.VMEM((base + 2 * extra, columns), jnp.float32),
            pltpu.VMEM((base, lent), jnp.bfloat16),
            pltpu.VMEM((lent, columns), jnp.bfloat16),
            pltpu.VMEM((extra, pieces[0].shape[1]), jnp.bfloat16),
        ],
        compiler_params=limit(8),
    )(flags, made, act, f_in, f_out, *pieces)


def score_kernel(spans, lengths_ref, *rest):
    arrays, out_ref = rest[:-1], rest[-1]
    columns, sequences = QUERIES * RANK, lengths_ref.shape[0]
    sums = [jnp.zeros((1, columns), jnp.float32) for _ in range(sequences)]
    for first, size, sides in spans:
        total = [
            sum(
                decode(arrays[which], at, size, column, columns)
                if arrays[which].dtype == jnp.int16
                else arrays[which][at : at + size, column : column + columns]
                for which, at, column in parts
            )
            for parts in sides
        ]
        product = total[0] * total[1]
        row = first + lax.broadcasted_iota(jnp.int32, (size, columns), 0)
        before = jnp.int32(0)
        for s in range(sequences):
            after = before + lengths_ref[s]
            mine = (row >= before) & (row < after)
            sums[s] += jnp.sum(jnp.where(mine, product, 0.0), axis=0, keepdims=True)
            before = after
    total = jnp.concatenate(sums, axis=0)
    out_ref[...] = jnp.concatenate(
        [jnp.sum(total[:, q * RANK : (q + 1) * RANK], axis=1, keepdims=True) for q in range(QUERIES)],
        axis=1,
    )


def score(spans, lengths, arrays):
    return pl.pallas_call(
        functools.partial(score_kernel, spans),
        out_shape=jax.ShapeDtypeStruct((lengths.shape[0], QUERIES), jnp.float32),
        in_specs=[SMEM] + [VMEM] * len(arrays),
        out_specs=VMEM,
        compiler_params=limit(4),
    )(lengths, *arrays)


def lendable(base, extra, columns, a_wide, g_wide):
    best = 0
    for lent in range(128, a_wide, 128):
        used = len(blocks_of(base, extra)) * lent + len(blocks_of(lent, extra)) * columns
        if used <= a_wide - lent + g_wide:
            best = lent
    return best


def swap(x):
    return lax.ppermute(x, "dp", SWAP)


def swapped_scores(rows, base, lent, chunks, flags, lengths, packed, act, grad, f_in, f_out):
    columns, extra = f_in.shape[1], rows - base
    first = swap(packed[:base, lent:])
    width = f_in.shape[0] - lent + f_out.shape[0]
    cuts = [width] if lent else [f_in.shape[0] + LEAD, f_out.shape[0] - LEAD]
    sent = rest_rows(chunks, extra, cuts, lent, flags, lengths, packed, f_in, grad)
    groups = list(zip(sent, [sum(chunks[:i]) for i in range(len(chunks))] + [base] * len(cuts)))
    if lent:
        x, at = groups.pop(1)
        groups += [(x[:, :-LEAD], at), (x[:, -LEAD:], at)]
    groups.sort(key=lambda group: -group[0].size)
    arrived = [swap(x) for x, _ in groups]
    made = first_project(lent, first, f_in)
    work = 0 if not lent else 1.7 if extra <= 3 * STEP else 2.9
    done = own = own_part(rows, lengths, act, grad, f_in, f_out, made, work)
    arrays, spans, in_parts = [own], [], [0]
    if not lent:
        in_parts.append(len(arrays))
        arrays.append(swap(made))
    for x, (_, at) in zip(arrived, groups):
        x, done = lax.optimization_barrier((x, done))
        here = len(arrays)
        if at < base and x.shape[1] == f_out.shape[0] - LEAD:
            done = begun = part(x, f_out)
            continue
        if at < base and x.shape[1] == LEAD:
            done = whole(x, begun, f_out)
            spans.append((at, x.shape[0], (here, 0, 0)))
        elif at < base:
            done = project(x, f_out)
            spans.append((at, x.shape[0], (here, 0, 0)))
        elif not lent and x.shape[1] == cuts[0]:
            done = begun = begin(x, f_in, f_out)
            continue
        elif not lent:
            done = finish(x, begun, f_out)
            spans.append((at, extra, (here, 0, columns)))
        else:
            done, added = extra_rows(lent, flags, made, [x], packed, f_in, f_out)
            in_parts += [here, here + 1]
            spans.append((at, extra, (here, rows, 0)))
        arrays.append(swap(done))
        if lent and at == base:
            arrays.append(added)
    spans = [
        (
            at,
            size,
            (
                ((0, at, 0), (back[0], 0, 0))
                if at == base and not lent
                else tuple((which, at, 0) for which in in_parts),
                ((0, at, columns), back),
            ),
        )
        for at, size, back in spans
    ]
    return score(spans, lengths, arrays)


def plan(rows, even, a_wide, g_wide, columns):
    if rows <= even + STEP:
        base = even - STEP
        large = (base + STEP) // 2 // STEP * STEP
        return rows, base, 0, [large, base - large]
    base = even - STEP
    large = (base + STEP) // 2 // STEP * STEP
    lent = lendable(base, rows - base, columns, a_wide, g_wide)
    return rows, base, lent, [large, base - large]


def layer_sum(x):
    size = lax.axis_size("layer")
    if size & (size - 1):
        return lax.psum(x, "layer")
    bits = [1 << i for i in range(size.bit_length() - 1)]
    steps = [bits[:1], bits[1:3], *([b] for b in bits[3:])]
    for step in steps:
        flips = [0]
        for bit in step:
            flips += [flip ^ bit for flip in flips]
        x = sum((lax.ppermute(x, "layer", [(i, i ^ flip) for i in range(size)]) for flip in flips[1:]), x)
    return x


def shards(activations, gradients, input_factor, output_factor, lengths):
    tokens = activations.shape[1]
    parts = lax.axis_size("dp")
    widths = (input_factor.shape[1], output_factor.shape[1])
    if parts == 2 and all(w % (2 * WIDE) == 0 for w in widths) and widths[1] > 2 * LEAD:
        act, grad, f_in, f_out = (x[0] for x in (activations, gradients, input_factor, output_factor))
        total = 5 * parts * tokens // 8
        even = (total // 2 + STEP - 1) // STEP * STEP
        sizes = [n for n in range(even, tokens, STEP) if n <= even + MOST * STEP] + [tokens]
        bounds = sizes[:-1]
        packed, flags = first_rows(total, bounds, lengths, act)
        plans = [plan(rows, even, *widths, f_in.shape[1]) for rows in sizes]
        per_sequence = lax.switch(
            flags[0],
            [functools.partial(swapped_scores, *p) for p in plans],
            *(flags, lengths, packed, act, grad, f_in, f_out),
        )
    else:
        per_sequence = gathered_scores(activations, gradients, input_factor, output_factor, lengths)
    blocks = lax.axis_size("layer")
    return layer_sum(per_sequence) / jnp.float32(math.sqrt(RANK * SLOT * blocks))


def solution(mesh):
    in_specs = (
        P("layer", "dp", None),
        P("layer", "dp", None),
        P("layer", "dp", None),
        P("layer", "dp", None),
        P("dp"),
    )
    out_specs = P("dp", None)
    return jax.shard_map(shards, mesh=mesh, in_specs=in_specs, out_specs=out_specs, check_vma=False)
```
